256 devices in a mesh: dp: 8 (over x_lo, y), seq: 32 (over x_hi, z, core).
Axes of the slice: x: 4 (x_hi: 2, x_lo: 2; x = x_hi * 2 + x_lo), y: 4, z: 8, core: 2. Of those that a mesh axis runs over, the one named last changes fastest.
Arguments:
- queries: bfloat16 [32768, 2048], P(('dp', 'seq')), may hold values from -12 to 12
- key_rows: bfloat16 [32768, 2048], P(('dp', 'seq')), may hold values from -12 to 12
- value_rows: bfloat16 [32768, 2048], P(('dp', 'seq')), may hold values from -6 to 6
- document_ids: int32 [8, 4096], P('dp'), may hold values from 0 to 31, never falling along the last dimension, each value on 1 to 512 neighbouring positions
- link_lists: int32 [8, 32, 8], P('dp'), may hold values from 0 to 31, as said below
- block_keep: int32 [8, 32, 32], P('dp'), may hold values 0 or 1
- out_gain: float32 [2048], replicated, may hold values from 0.1 to 1.9
- cotangent: bfloat16 [32768, 2048], P(('dp', 'seq')), may hold values from -0.25 to 0.25
Outputs:
- attended: bfloat16 [32768, 2048], P(('dp', 'seq'))
- gain_grad: float32 [2048], P(('dp', 'seq'))
The draws below stay inside these ranges and needn't reach their ends.
Inputs may be any that keep to these rules, and one draw needn't show every extreme that they name: `link_lists`: each target document lies within 3 documents of its source.
All inputs are finite; a program needn't handle non-finite values. No bound on the sum of `block_keep` on one device may be relied on, other than what follows from the above.
Results may differ from the reference program's by a relative error of at most 0.0035.
Values may be sent and summed in bfloat16 or wider, within the bound.
No kernel may reach another device: no remote copies, remote signals or barrier semaphores. Data moves between devices by JAX's collectives and lax.ppermute only.
A program may use at most 64 MiB of HBM per device.

```python
import math
import jax
import jax.numpy as jnp
import numpy as np
from jax import lax

HEADS = 32
HDIM = 64
TOK_DEV = 128
REACH = 3
BLK = 128
LINKS = 8
CH = 2048
PACKS = 8
SEQ = 4096
TOKENS = 32768
NDOC = 32
NBLK = 32
SPREAD = 3
DOC_MOST = 512


def spread_rows(key):
    logs = jax.random.uniform(key, (TOKENS, 1), jnp.float32, math.log(0.3), math.log(3.0))
    return jnp.exp(logs)


def draw_queries(key, part):
    key = jax.random.fold_in(key, 5)
    first_key, second_key = jax.random.split(key)
    row_scale = spread_rows(second_key)
    entries = jax.random.normal(first_key, (TOKENS, CH), jnp.float32) * row_scale
    return jnp.clip(entries, -12.0, 12.0).astype(jnp.bfloat16)


def draw_key_rows(key, part):
    key = jax.random.fold_in(key, 6)
    first_key, second_key = jax.random.split(key)
    row_scale = spread_rows(second_key)
    entries = jax.random.normal(first_key, (TOKENS, CH), jnp.float32) * row_scale
    return jnp.clip(entries, -12.0, 12.0).astype(jnp.bfloat16)


def draw_link_lists(key, part):
    key = jax.random.fold_in(key, 7)
    source_docs = jnp.arange(NDOC, dtype=jnp.int32)[None, :, None]
    offsets = jax.random.randint(key, (PACKS, NDOC, LINKS), -SPREAD, SPREAD + 1, dtype=jnp.int32)
    targets = jnp.clip(source_docs + offsets, 0, NDOC - 1)
    targets = targets.at[:, 0, 0].set(0)
    targets = targets.at[:, NDOC - 1, 0].set(NDOC - 1)
    return targets.astype(jnp.int32)


def set_ends(values, own_key, smallest, top_value):
    shape = values.shape
    place = [jax.random.randint(jax.random.fold_in(own_key, axis), (), 0, shape[axis]) for axis in range(len(shape))]
    values = values.at[tuple(place)].set(smallest)
    longest = shape.index(max(shape))
    place[longest] = (place[longest] + 1) % shape[longest]
    return values.at[tuple(place)].set(top_value)


def with_spikes(values, rng, source, target, parts, factor):
    def block_of(position):
        return (jnp.arange(values.shape[position]) // (values.shape[position] // parts)).reshape((-1,) + (1,) * (values.ndim - 1 - position))

    first = jax.random.permutation(rng, parts)[block_of(target)]
    second = (block_of(target) + parts // 2) % parts
    return jnp.where((block_of(source) == first) | (block_of(source) == second), factor * values, values)


def block_scale(stream_key, dims, pieces, smallest, largest):
    gain = 1.0
    for axis_at, shards_of in pieces:
        steps = jax.random.uniform(jax.random.fold_in(jax.random.fold_in(stream_key, 6), axis_at), (shards_of,), jnp.float32, smallest / len(pieces), largest / len(pieces))
        gain = gain * jnp.repeat(jnp.exp(steps), dims[axis_at] // shards_of).reshape((-1,) + (1,) * (len(dims) - 1 - axis_at))
    return gain


def split_up(number_of, total, most, slope):
    portions = [(1 << 20) // math.isqrt(standing ** slope) + 1 for standing in range(2, number_of + 1)]
    surplus, counts = total - most - (number_of - 1), [1] * (number_of - 1)
    while surplus > 0:
        free = [i for i in range(number_of - 1) if counts[i] < most]
        whole, remaining = sum([portions[i] for i in free]), surplus
        for i in free:
            addition = min(most - counts[i], max(1, remaining * portions[i] // whole), surplus)
            counts[i] = counts[i] + addition
            surplus = surplus - addition
    return np.array([most] + counts)


def uneven_parts(rng, amount, total, reach, lean):
    if amount == 2:
        one = jax.random.randint(rng, (), max(1, total - reach), min(reach, total - 1) + 1)
        return jnp.stack([one, total - one])
    lengths = jnp.asarray(split_up(amount, total, reach, lean), jnp.int32)
    twos = (amount - 1) // 2
    donor, sink = lengths[1:1 + 2 * twos:2], lengths[2:2 + 2 * twos:2]
    slack = jnp.minimum(donor - 1, reach - sink)
    shifted = jax.random.randint(jax.random.fold_in(rng, 1), (twos,), 0, 1 << 20) % (slack + 1)
    lengths = lengths.at[1:1 + 2 * twos:2].set(donor - shifted).at[2:2 + 2 * twos:2].set(sink + shifted)
    return lengths[jax.random.permutation(jax.random.fold_in(rng, 2), amount)]


def normal_values(rng, dims, width, bound, cuts=(), held_as=jnp.bfloat16):
    drawn = width * jax.random.normal(rng, dims, jnp.float32)
    if cuts:
        drawn = drawn * block_scale(rng, dims, cuts, -0.22, 0.18)
    return jnp.clip(drawn, -bound, bound).astype(held_as)


def gaussian_with(own_key, shape, scale, bound, pieces, heavy, kind=jnp.bfloat16):
    drawn = scale * jax.random.normal(own_key, shape, jnp.float32)
    if pieces:
        drawn = drawn * block_scale(own_key, shape, pieces, -0.22, 0.18)
    return jnp.clip(with_spikes(drawn, jax.random.fold_in(own_key, 3), *heavy), -bound, bound).astype(kind)


def setup_inputs(seed: int = 0) -> dict:
    splits = jax.random.split(jax.random.key(seed), 9)
    return {
        "queries": draw_queries(jax.random.fold_in(splits[8], 71), 0),
        "key_rows": draw_key_rows(jax.random.fold_in(splits[8], 71), 0),
        "value_rows": normal_values(splits[2], (TOKENS, CH), 1.0, 6.0, ((0, 256),)),
        "document_ids": jax.vmap(lambda own: jnp.searchsorted(jnp.cumsum(uneven_parts(own, NDOC, SEQ, DOC_MOST, 1)), jnp.arange(SEQ), side="right"))(jax.random.split(splits[3], PACKS)).reshape((PACKS, SEQ)).astype(jnp.int32),
        "link_lists": draw_link_lists(jax.random.fold_in(splits[8], 71), 0),
        "block_keep": set_ends((jax.random.randint(splits[5], (PACKS, NBLK, NBLK), 0, 4) < 3).astype(jnp.int32), jax.random.fold_in(splits[5], 1), 0, 1),
        "out_gain": jnp.clip(1.0 + 0.18 * jax.random.normal(splits[6], (CH,), jnp.float32), 0.1, 1.9),
        "cotangent": gaussian_with(splits[7], (TOKENS, CH), 0.01, 0.25, ((0, 256),), (0, 1, 256, 6.0)),
    }


NEGATIVE_FILL = -1e+30

def pack_attention(queries, key_rows, value_rows, documents, links, keep):
    window = REACH * TOK_DEV
    span = TOK_DEV + 2 * window
    score_scale = 1.0 / math.sqrt(HDIM)
    key_pad = jnp.pad(key_rows, ((window, window), (0, 0)))
    value_pad = jnp.pad(value_rows, ((window, window), (0, 0)))
    doc_pad = jnp.pad(documents, (window, window), constant_values=-1)

    def one_block(block_index):
        first_row = (block_index * TOK_DEV).astype(jnp.int32)
        query_pos = first_row + jnp.arange(TOK_DEV, dtype=jnp.int32)
        key_pos = first_row - window + jnp.arange(span, dtype=jnp.int32)
        query_block = lax.dynamic_slice_in_dim(queries, first_row, TOK_DEV, 0).astype(jnp.float32).reshape(TOK_DEV, HEADS, HDIM)
        key_block = lax.dynamic_slice_in_dim(key_pad, first_row, span, 0).astype(jnp.float32).reshape(span, HEADS, HDIM)
        value_block = lax.dynamic_slice_in_dim(value_pad, first_row, span, 0).astype(jnp.float32).reshape(span, HEADS, HDIM)
        query_docs = lax.dynamic_slice_in_dim(documents, first_row, TOK_DEV, 0)
        key_docs = lax.dynamic_slice_in_dim(doc_pad, first_row, span, 0)
        query_links = links[query_docs]
        linked = jnp.any(query_links[:, :, None] == key_docs[None, None, :], axis=1)
        same_doc = query_docs[:, None] == key_docs[None, :]
        inside = (key_pos >= 0) & (key_pos < SEQ)
        in_window = jnp.abs(query_pos[:, None] - key_pos[None, :]) <= window
        block_bits = keep[query_pos // BLK][:, jnp.clip(key_pos, 0, SEQ - 1) // BLK] == 1
        allowed = inside[None, :] & in_window & (same_doc | linked & block_bits)
        scores = jnp.einsum('thd,uhd->htu', query_block, key_block) * score_scale
        masked = jnp.where(allowed[None], scores, NEGATIVE_FILL)
        maxima = lax.optimization_barrier(jnp.max(masked, axis=-1))
        expo = jnp.where(allowed[None], jnp.exp(masked - maxima[..., None]), 0.0)
        totals = lax.optimization_barrier(jnp.sum(expo, axis=-1))
        weights = lax.optimization_barrier(expo.astype(jnp.bfloat16))
        product = jnp.einsum('htu,uhd->thd', weights.astype(jnp.float32), value_block)
        mixed = product / jnp.transpose(totals)[:, :, None]
        return mixed.reshape(TOK_DEV, HEADS * HDIM)
    blocks = lax.map(one_block, jnp.arange(SEQ // TOK_DEV, dtype=jnp.int32))
    return blocks.reshape(SEQ, HEADS * HDIM)

def reference(queries, key_rows, value_rows, document_ids, link_lists, block_keep, out_gain, cotangent):
    channels = HEADS * HDIM

    def one_pack(items):
        return pack_attention(items[0], items[1], items[2], items[3], items[4], items[5])
    stacked = lax.map(one_pack, (queries.reshape(PACKS, SEQ, channels), key_rows.reshape(PACKS, SEQ, channels), value_rows.reshape(PACKS, SEQ, channels), document_ids, link_lists, block_keep))
    mixed = stacked.reshape(TOKENS, channels)
    attended = (out_gain * mixed).astype(jnp.bfloat16)
    gain_grad = lax.optimization_barrier(jnp.sum(mixed * cotangent.astype(jnp.float32), axis=0))
    return (attended, gain_grad)
```

```python
import functools
import math

import jax
import jax.numpy as jnp
from jax import lax
from jax.experimental import pallas as pl
from jax.experimental.pallas import tpu as pltpu
from jax.sharding import PartitionSpec as P

HEADS = 32
HDIM = 64
REACH = 3
BLK = 128
HALF = HEADS * HDIM // 2
PAIRS = HALF // 128
NEGATIVE_FILL = -1e30
AXES = ("dp", "seq")


def prep_kernel(core_ref, a_own, b_own, a_other, b_other, own_ref, send_ref):
    own_ref[:BLK] = a_own[...]
    own_ref[BLK:] = b_own[...]
    send_ref[:BLK] = a_other[...]
    send_ref[BLK:] = b_other[...]


def split_heads(core, a, b):
    steps = 2
    width = HALF // steps
    mine = pl.BlockSpec((BLK, width), lambda i, c: (0, c[0] * steps + i))
    others = pl.BlockSpec((BLK, width), lambda i, c: (0, (1 - c[0]) * steps + i))
    out = pl.BlockSpec((2 * BLK, width), lambda i, c: (0, i))
    shape = jax.ShapeDtypeStruct((2 * BLK, HALF), a.dtype)
    return pl.pallas_call(
        prep_kernel,
        grid_spec=pltpu.PrefetchScalarGridSpec(
            num_scalar_prefetch=1, grid=(steps,), in_specs=[mine, mine, others, others], out_specs=[out, out]
        ),
        out_shape=[shape, shape],
        cost_estimate=pl.CostEstimate(flops=0, bytes_accessed=4 << 20, transcendentals=0),
    )(core, a, b, a, b)


OWN, SIB, R1, R2, R3, R4, R5, R6 = range(8)
TILES = (
    [(q, k) for q in (OWN, SIB) for k in (OWN, SIB)]
    + [(q, k) for q in (OWN, SIB) for k in (R1, R2)]
    + [(q, k) for q in (OWN, SIB) for k in (R3, R4)]
    + [(SIB, R5), (OWN, R6)]
)


def mask_kernel(blocks_ref, keep_ref, docs_ref, links_ref, bias_ref):
    docs_in_pack = links_ref.shape[0]
    nblk = docs_ref.shape[1] // BLK
    target = lax.broadcasted_iota(jnp.int32, (docs_in_pack, docs_in_pack), 1)
    source = lax.broadcasted_iota(jnp.int32, (docs_in_pack, docs_in_pack), 0)
    linked = target == links_ref[:, 0:1]
    for at in range(1, links_ref.shape[1]):
        linked = linked | (target == links_ref[:, at : at + 1])
    table = jnp.where(source == target, 2.0, 0.0) + jnp.where(linked, 1.0, 0.0)
    table = table.astype(jnp.bfloat16)

    def one_hot(block):
        at = pl.multiple_of(jnp.clip(block, 0, nblk - 1) * BLK, BLK)
        row = docs_ref[:, pl.ds(at, BLK)]
        rows = lax.broadcasted_iota(jnp.int32, (docs_in_pack, BLK), 0)
        return jnp.where(rows == row, 1.0, 0.0).astype(jnp.bfloat16)

    hots = [one_hot(blocks_ref[place]) for place in range(8)]
    related = [
        lax.dot_general(table, hots[q], (((0,), (0,)), ((), ())), preferred_element_type=jnp.float32).astype(jnp.bfloat16)
        for q in (OWN, SIB)
    ]
    key_at = lax.broadcasted_iota(jnp.int32, (BLK, BLK), 0)
    query_at = lax.broadcasted_iota(jnp.int32, (BLK, BLK), 1)
    apart = query_at - key_at
    for tile, (q, k) in enumerate(TILES):
        query_block, key_block = blocks_ref[q], blocks_ref[k]
        present = (key_block >= 0) & (key_block < nblk)
        kept = keep_ref[query_block * nblk + jnp.clip(key_block, 0, nblk - 1)] == 1
        least = jnp.where(present, jnp.where(kept, 0.5, 1.5), 9.0)
        relation = lax.dot_general(hots[k], related[q], (((0,), (0,)), ((), ())), preferred_element_type=jnp.float32)
        distance = apart + (query_block - key_block) * BLK
        allowed = (relation > least) & (jnp.abs(distance) <= REACH * BLK)
        bias_ref[tile * BLK : (tile + 1) * BLK] = jnp.where(allowed, 0.0, NEGATIVE_FILL)


def masks(blocks, keep, docs, links):
    whole = lambda shape: pl.BlockSpec(shape, lambda i, *_: (0,) * len(shape))
    return pl.pallas_call(
        mask_kernel,
        grid_spec=pltpu.PrefetchScalarGridSpec(
            num_scalar_prefetch=2,
            grid=(1,),
            in_specs=[whole(docs.shape), whole(links.shape)],
            out_specs=whole((len(TILES) * BLK, BLK)),
        ),
        out_shape=jax.ShapeDtypeStruct((len(TILES) * BLK, BLK), jnp.float32),
        cost_estimate=pl.CostEstimate(flops=1 << 20, bytes_accessed=2 << 20, transcendentals=0),
    )(blocks, keep, docs, links)


def absorb(query, keys, values, bias, state):
    low = lax.broadcasted_iota(jnp.int32, query.shape, 1) < HDIM
    scaled = query * jnp.bfloat16(1.0 / math.sqrt(HDIM))
    nothing = jnp.zeros_like(scaled)
    both = jnp.concatenate([jnp.where(low, scaled, nothing), jnp.where(low, nothing, scaled)], axis=0)
    scores = lax.dot_general(keys, both, (((1,), (1,)), ((), ())), preferred_element_type=jnp.float32)
    scores = scores + jnp.concatenate([bias, bias], axis=1)
    largest = jnp.max(scores, axis=0, keepdims=True)
    if state is not None:
        largest = jnp.maximum(state[0], largest)
    expo = jnp.exp(scores - largest)
    totals = jnp.sum(expo, axis=0, keepdims=True)
    sums = lax.dot_general(
        values, expo.astype(jnp.bfloat16), (((0,), (0,)), ((), ())), preferred_element_type=jnp.float32
    )
    folded = jnp.concatenate([sums[:HDIM, :BLK], sums[HDIM:, BLK:]], axis=0)
    if state is not None:
        shrink = jnp.exp(state[0] - largest)
        totals = totals + state[1] * shrink
        folded = folded + state[2] * spread(shrink)
    return largest, totals, folded


def spread(row):
    first = jnp.broadcast_to(row[:, :BLK], (HDIM, BLK))
    second = jnp.broadcast_to(row[:, BLK:], (HDIM, BLK))
    return jnp.concatenate([first, second], axis=0)


def put_state(rows_ref, sums_ref, state):
    rows_ref[0:1] = state[0]
    rows_ref[1:2] = state[1]
    sums_ref[...] = state[2]


def first_kernel(bias_ref, qc_own, qc_sib, kv_a, kv_b, rows_own, sums_own, rows_sib, sums_sib):
    keys = jnp.concatenate([kv_a[:BLK], kv_b[:BLK]], axis=0)
    values = jnp.concatenate([kv_a[BLK:], kv_b[BLK:]], axis=0)
    put_state(rows_own, sums_own, absorb(qc_own[:BLK], keys, values, bias_ref[: 2 * BLK], None))
    put_state(rows_sib, sums_sib, absorb(qc_sib[:BLK], keys, values, bias_ref[2 * BLK :], None))


def middle_kernel(bias_ref, qc_own, qc_sib, kv_a, kv_b, ro, so, rs, ss, rows_own, sums_own, rows_sib, sums_sib):
    keys = jnp.concatenate([kv_a[:BLK], kv_b[:BLK]], axis=0)
    values = jnp.concatenate([kv_a[BLK:], kv_b[BLK:]], axis=0)
    state = (ro[0:1], ro[1:2], so[...])
    put_state(rows_own, sums_own, absorb(qc_own[:BLK], keys, values, bias_ref[: 2 * BLK], state))
    state = (rs[0:1], rs[1:2], ss[...])
    put_state(rows_sib, sums_sib, absorb(qc_sib[:BLK], keys, values, bias_ref[2 * BLK :], state))


def finish(state, gain, cotangent):
    mixed = jnp.transpose(state[2] / spread(state[1]))
    attended = (gain * mixed).astype(jnp.bfloat16)
    terms = jnp.sum(mixed * cotangent.astype(jnp.float32), axis=0, keepdims=True)
    return attended, terms


def sib_kernel(core_ref, bias_ref, qc, kv, rows, sums, gain_ref, att_ref, terms_ref):
    state = absorb(qc[:BLK], kv[:BLK], kv[BLK:], bias_ref[...], (rows[0:1], rows[1:2], sums[...]))
    att_ref[...], terms = finish(state, gain_ref[...], qc[BLK:])
    terms_ref[...] = jnp.broadcast_to(terms, terms_ref.shape)


def own_kernel(core_ref, bias_ref, qc, kv, rows, sums, gain_ref, terms_in, back, out_ref, terms_ref):
    state = absorb(qc[:BLK], kv[:BLK], kv[BLK:], bias_ref[...], (rows[0:1], rows[1:2], sums[...]))
    attended, terms = finish(state, gain_ref[...], qc[BLK:])
    core = core_ref[0]
    at = pl.program_id(0)
    out_ref[:, pl.ds(pl.multiple_of(core * HALF + at * BLK, BLK), BLK)] = attended
    out_ref[:, pl.ds(pl.multiple_of((1 - core) * HALF + at * BLK, BLK), BLK)] = back[...]

    @pl.when(at == 0)
    def _():
        terms_ref[...] = jnp.zeros_like(terms_ref)

    terms_ref[pl.ds(core * PAIRS + at, 1), :] = terms + terms_in[0:1]


ROWS = pl.BlockSpec((8, 2 * BLK), lambda j, *_: (j, 0))
SUMS = pl.BlockSpec((BLK, BLK), lambda j, *_: (j, 0))
COLS = pl.BlockSpec((2 * BLK, BLK), lambda j, *_: (0, j))
ONE = pl.BlockSpec((BLK, BLK), lambda j, *_: (0, j))
STATE = [
    jax.ShapeDtypeStruct((PAIRS * 8, 2 * BLK), jnp.float32),
    jax.ShapeDtypeStruct((PAIRS * BLK, BLK), jnp.float32),
]


def bias_at(tiles, place):
    return pl.BlockSpec((tiles * BLK, BLK), lambda j, *_: (place, 0))


def cost(tiles):
    return pl.CostEstimate(
        flops=tiles * 16 * 4 * BLK * BLK * HDIM, bytes_accessed=4 << 20, transcendentals=tiles * 16 * BLK * BLK
    )


def first(bias, qc_own, qc_sib, kv_a, kv_b):
    return pl.pallas_call(
        first_kernel,
        grid=(PAIRS,),
        in_specs=[bias_at(4, 0), COLS, COLS, COLS, COLS],
        out_specs=[ROWS, SUMS, ROWS, SUMS],
        out_shape=STATE + STATE,
        cost_estimate=cost(4),
    )(bias, qc_own, qc_sib, kv_a, kv_b)


def middle(place, bias, qc_own, qc_sib, kv_a, kv_b, state):
    return pl.pallas_call(
        middle_kernel,
        grid=(PAIRS,),
        in_specs=[bias_at(4, place), COLS, COLS, COLS, COLS, ROWS, SUMS, ROWS, SUMS],
        out_specs=[ROWS, SUMS, ROWS, SUMS],
        out_shape=STATE + STATE,
        cost_estimate=cost(4),
    )(bias, qc_own, qc_sib, kv_a, kv_b, *state)


def last_sib(core, bias, qc, kv, rows, sums, gain):
    return pl.pallas_call(
        sib_kernel,
        grid_spec=pltpu.PrefetchScalarGridSpec(
            num_scalar_prefetch=1,
            grid=(PAIRS,),
            in_specs=[bias_at(1, 12), COLS, COLS, ROWS, SUMS, pl.BlockSpec((1, BLK), lambda j, c: (0, c[0] * PAIRS + j))],
            out_specs=[ONE, pl.BlockSpec((8, BLK), lambda j, c: (j, 0))],
        ),
        out_shape=[
            jax.ShapeDtypeStruct((BLK, HALF), jnp.bfloat16),
            jax.ShapeDtypeStruct((PAIRS * 8, BLK), jnp.float32),
        ],
        cost_estimate=cost(1),
    )(core, bias, qc, kv, rows, sums, gain)


def last_own(core, bias, qc, kv, rows, sums, gain, terms, back):
    return pl.pallas_call(
        own_kernel,
        grid_spec=pltpu.PrefetchScalarGridSpec(
            num_scalar_prefetch=1,
            grid=(PAIRS,),
            in_specs=[
                bias_at(1, 13),
                COLS,
                COLS,
                ROWS,
                SUMS,
                pl.BlockSpec((1, BLK), lambda j, c: (0, c[0] * PAIRS + j)),
                pl.BlockSpec((8, BLK), lambda j, c: (j, 0)),
                ONE,
            ],
            out_specs=[
                pl.BlockSpec((BLK, 2 * HALF), lambda j, c: (0, 0)),
                pl.BlockSpec((2 * PAIRS, BLK), lambda j, c: (0, 0)),
            ],
        ),
        out_shape=[
            jax.ShapeDtypeStruct((BLK, 2 * HALF), jnp.bfloat16),
            jax.ShapeDtypeStruct((2 * PAIRS, BLK), jnp.float32),
        ],
        cost_estimate=cost(1),
    )(core, bias, qc, kv, rows, sums, gain, terms, back)


def rotations(groups, shards):
    onward = []
    for group in range(groups):
        for place in range(shards):
            chip, core = divmod(place, 2)
            there = chip + (1 if core == 1 else -1)
            target = there * 2 + core if 0 <= there < shards // 2 else chip * 2 + 1 - core
            onward.append((group * shards + place, group * shards + target))
    return onward, [(target, source) for source, target in onward]


def after(value, *others):
    return lax.optimization_barrier((value, *others))[0]


def local(queries, key_rows, value_rows, document_ids, link_lists, block_keep, out_gain, cotangent):
    groups, shards = lax.axis_size("dp"), lax.axis_size("seq")
    place = lax.axis_index("seq")
    chip, core = place // 2, place % 2
    toward = 1 - 2 * core
    chips = jnp.stack([chip, chip, chip + toward, chip - toward, chip - toward, chip + toward, chip + 2 * toward, chip - 2 * toward])
    cores = jnp.stack([core, 1 - core, core, 1 - core, core, 1 - core, core, 1 - core])
    blocks = jnp.where((chips >= 0) & (chips < shards // 2), 2 * chips + cores, -1).astype(jnp.int32)
    core_at = core.reshape(1).astype(jnp.int32)
    onward, backward = rotations(groups, shards)
    siblings = [(i, i ^ 1) for i in range(groups * shards)]
    move = lambda value, pairs: lax.ppermute(value, AXES, pairs)
    gain = out_gain.reshape(1, -1)

    kv_own, kv_send = split_heads(core_at, key_rows, value_rows)
    kv_sib = move(kv_send, siblings)
    r1 = move(kv_own, onward)
    r2 = move(kv_sib, backward)
    r3 = move(after(kv_own, r1), backward)
    r5 = move(after(r1, r2), onward)
    r4 = move(after(kv_sib, r3), onward)
    r6 = move(after(r2, r5), backward)

    qc_own, qc_send = split_heads(core_at, queries, cotangent)
    qc_sib = move(qc_send, siblings)
    bias = masks(blocks, block_keep.reshape(-1), document_ids, link_lists[0])

    state = first(bias, qc_own, qc_sib, kv_own, kv_sib)
    state = middle(1, bias, qc_own, qc_sib, r1, r2, state)
    state = middle(2, bias, qc_own, qc_sib, r3, r4, state)
    att_sib, terms = last_sib(core_at, bias, qc_sib, r5, state[2], state[3], gain)
    back = move(att_sib, siblings)
    attended, terms = last_own(core_at, bias, qc_own, r6, state[0], state[1], gain, terms, back)
    pieces = lax.all_to_all(terms.reshape(groups * shards, -1), AXES, 0, 0, tiled=True)
    return attended, jnp.sum(pieces, axis=0)


def solution(mesh):
    placed = (
        P(AXES, None),
        P(AXES, None),
        P(AXES, None),
        P("dp", None),
        P("dp", None, None),
        P("dp", None, None),
        P(),
        P(AXES, None),
    )
    return jax.shard_map(local, mesh=mesh, in_specs=placed, out_specs=(P(AXES, None), P(AXES)), check_vma=False)
```

```python
import functools
import math

import jax
import jax.numpy as jnp
from jax import lax
from jax.experimental import pallas as pl
from jax.experimental.pallas import tpu as pltpu
from jax.sharding import PartitionSpec as P

HEADS = 32
HDIM = 64
REACH = 3
BLK = 128
HALF = HEADS * HDIM // 2
PAIRS = HALF // 128
NEGATIVE_FILL = -1e30
AXES = ("dp", "seq")


def split_kernel(a_ref, b_ref, own_ref, send_ref, sems):
    core = lax.axis_index("seq") % 2
    copies = []
    for side, out_ref in enumerate((own_ref, send_ref)):
        at = pl.multiple_of((core if side == 0 else 1 - core) * HALF, HALF)
        for part, ref in enumerate((a_ref, b_ref)):
            source = ref.at[:, pl.ds(at, HALF)]
            copies.append(pltpu.make_async_copy(source, out_ref.at[cols(part)], sems.at[side, part]))
    for copy in copies:
        copy.start()
    for copy in copies:
        copy.wait()


def split_heads(a, b):
    shape = pltpu.VMEM((2 * BLK, HALF), a.dtype)
    return pl.pallas_call(
        split_kernel,
        in_specs=[pl.BlockSpec(memory_space=pl.ANY)] * 2,
        out_specs=[pl.BlockSpec(memory_space=pltpu.VMEM)] * 2,
        out_shape=[shape, shape],
        scratch_shapes=[pltpu.SemaphoreType.DMA((2, 2))],
        cost_estimate=pl.CostEstimate(flops=0, bytes_accessed=2 << 20, transcendentals=0),
    )(a, b)


OWN, SIB, R1, R2, R3, R4, R5, R6 = range(8)
TILES = (
    [(q, k) for q in (OWN, SIB) for k in (OWN, SIB)]
    + [(q, k) for q in (OWN, SIB) for k in (R1, R2)]
    + [(q, k) for q in (OWN, SIB) for k in (R3, R4)]
    + [(SIB, R5), (OWN, R6)]
)


def key_blocks():
    place = lax.axis_index("seq")
    chip, core = place // 2, place % 2
    toward = 1 - 2 * core
    ring = [(chip, core), (chip, 1 - core)]
    ring += [(chip + toward, core), (chip - toward, 1 - core), (chip - toward, core), (chip + toward, 1 - core)]
    ring += [(chip + 2 * toward, core), (chip - 2 * toward, 1 - core)]
    return [2 * at + side for at, side in ring]


def mask_kernel(keep_ref, docs_ref, links_ref, bias_ref):
    docs_in_pack = links_ref.shape[1]
    nblk = docs_ref.shape[1] // BLK
    blocks = key_blocks()
    target = lax.broadcasted_iota(jnp.int32, (docs_in_pack, docs_in_pack), 1)
    source = lax.broadcasted_iota(jnp.int32, (docs_in_pack, docs_in_pack), 0)
    links = links_ref[0]
    linked = target == links[:, 0:1]
    for at in range(1, links.shape[1]):
        linked = linked | (target == links[:, at : at + 1])
    table = jnp.where(source == target, 2.0, 0.0) + jnp.where(linked, 1.0, 0.0)
    table = table.astype(jnp.bfloat16)

    def one_hot(block):
        at = pl.multiple_of(jnp.clip(block, 0, nblk - 1) * BLK, BLK)
        row = docs_ref[:, pl.ds(at, BLK)]
        rows = lax.broadcasted_iota(jnp.int32, (docs_in_pack, BLK), 0)
        return jnp.where(rows == row, 1.0, 0.0).astype(jnp.bfloat16)

    hots = [one_hot(block) for block in blocks]
    related = [
        lax.dot_general(table, hots[q], (((0,), (0,)), ((), ())), preferred_element_type=jnp.float32).astype(jnp.bfloat16)
        for q in (OWN, SIB)
    ]
    key_at = lax.broadcasted_iota(jnp.int32, (BLK, BLK), 0)
    query_at = lax.broadcasted_iota(jnp.int32, (BLK, BLK), 1)
    apart = query_at - key_at
    for tile, (q, k) in enumerate(TILES):
        query_block, key_block = blocks[q], blocks[k]
        present = (key_block >= 0) & (key_block < nblk)
        kept = keep_ref[0, query_block, jnp.clip(key_block, 0, nblk - 1)] == 1
        least = jnp.where(present, jnp.where(kept, 0.5, 1.5), 9.0)
        relation = lax.dot_general(hots[k], related[q], (((0,), (0,)), ((), ())), preferred_element_type=jnp.float32)
        distance = apart + (query_block - key_block) * BLK
        allowed = (relation > least) & (jnp.abs(distance) <= REACH * BLK)
        bias_ref[tile * BLK : (tile + 1) * BLK] = jnp.where(allowed, 0.0, NEGATIVE_FILL)


def masks(keep, docs, links):
    return in_vmem(mask_kernel, 1, [pltpu.VMEM((len(TILES) * BLK, BLK), jnp.float32)], keep, docs, links, scalars=1)[0]


def absorb(query, keys, values, bias, state):
    low = lax.broadcasted_iota(jnp.int32, query.shape, 1) < HDIM
    scaled = query * jnp.bfloat16(1.0 / math.sqrt(HDIM))
    nothing = jnp.zeros_like(scaled)
    both = jnp.concatenate([jnp.where(low, scaled, nothing), jnp.where(low, nothing, scaled)], axis=0)
    scores = lax.dot_general(keys, both, (((1,), (1,)), ((), ())), preferred_element_type=jnp.float32)
    scores = scores + jnp.concatenate([bias, bias], axis=1)
    largest = jnp.max(scores, axis=0, keepdims=True)
    if state is not None:
        largest = jnp.maximum(state[0], largest)
    expo = jnp.exp(scores - largest)
    totals = jnp.sum(expo, axis=0, keepdims=True)
    sums = lax.dot_general(
        values, expo.astype(jnp.bfloat16), (((0,), (0,)), ((), ())), preferred_element_type=jnp.float32
    )
    folded = jnp.concatenate([sums[:HDIM, :BLK], sums[HDIM:, BLK:]], axis=0)
    if state is not None:
        shrink = jnp.exp(state[0] - largest)
        totals = totals + state[1] * shrink
        folded = folded + state[2] * spread(shrink)
    return largest, totals, folded


def spread(row):
    first = jnp.broadcast_to(row[:, :BLK], (HDIM, BLK))
    second = jnp.broadcast_to(row[:, BLK:], (HDIM, BLK))
    return jnp.concatenate([first, second], axis=0)


def cols(at):
    return slice(at * BLK, (at + 1) * BLK)


def get_state(rows_ref, sums_ref, at):
    return rows_ref[at * 8 : at * 8 + 1], rows_ref[at * 8 + 1 : at * 8 + 2], sums_ref[cols(at)]


def put_state(rows_ref, sums_ref, at, state):
    rows_ref[at * 8 : at * 8 + 1] = state[0]
    rows_ref[at * 8 + 1 : at * 8 + 2] = state[1]
    sums_ref[cols(at)] = state[2]


def both_kernel(tile, bias_ref, qc_own, qc_sib, kv_a, kv_b, *states):
    before, now = states[:-4], states[-4:]
    for at in range(PAIRS):
        at_cols = cols(at)
        keys = jnp.concatenate([kv_a[:BLK, at_cols], kv_b[:BLK, at_cols]], axis=0)
        values = jnp.concatenate([kv_a[BLK:, at_cols], kv_b[BLK:, at_cols]], axis=0)
        for side, qc in enumerate((qc_own, qc_sib)):
            bias = bias_ref[(tile + 2 * side) * BLK : (tile + 2 * side + 2) * BLK]
            state = get_state(*before[2 * side : 2 * side + 2], at) if before else None
            put_state(*now[2 * side : 2 * side + 2], at, absorb(qc[:BLK, at_cols], keys, values, bias, state))


def finish(state, gain, cotangent):
    mixed = jnp.transpose(state[2] / spread(state[1]))
    attended = (gain * mixed).astype(jnp.bfloat16)
    terms = jnp.sum(mixed * cotangent.astype(jnp.float32), axis=0, keepdims=True)
    return attended, terms


def last(tile, at, bias_ref, qc, kv, rows, sums, gain_ref):
    at_cols = cols(at)
    core = lax.axis_index("seq") % 2
    bias = bias_ref[cols(tile)]
    state = absorb(qc[:BLK, at_cols], kv[:BLK, at_cols], kv[BLK:, at_cols], bias, get_state(rows, sums, at))
    gain = gain_ref[:, pl.ds(pl.multiple_of(core * HALF + at * BLK, BLK), BLK)]
    return finish(state, gain, qc[BLK:, at_cols])


def sib_kernel(bias_ref, qc, kv, rows, sums, gain_ref, att_ref, terms_ref):
    for at in range(PAIRS):
        att_ref[:, cols(at)], terms = last(12, at, bias_ref, qc, kv, rows, sums, gain_ref)
        terms_ref[at : at + 1] = terms


def own_kernel(bias_ref, qc, kv, rows, sums, gain_ref, terms_in, back, out_ref, terms_ref):
    core = lax.axis_index("seq") % 2
    terms_ref[...] = jnp.zeros_like(terms_ref)
    for at in range(PAIRS):
        attended, terms = last(13, at, bias_ref, qc, kv, rows, sums, gain_ref)
        out_ref[:, pl.ds(pl.multiple_of(core * HALF + at * BLK, BLK), BLK)] = attended
        out_ref[:, pl.ds(pl.multiple_of((1 - core) * HALF + at * BLK, BLK), BLK)] = back[:, cols(at)]
        terms_ref[pl.ds(core * PAIRS + at, 1), :] = terms + terms_in[at : at + 1]


STATE = [pltpu.VMEM((PAIRS * 8, 2 * BLK), jnp.float32), pltpu.VMEM((PAIRS * BLK, BLK), jnp.float32)]


def in_vmem(kernel, tiles, outputs, *operands, scalars=0):
    vmem = pl.BlockSpec(memory_space=pltpu.VMEM)
    smem = pl.BlockSpec(memory_space=pltpu.SMEM)
    cost = pl.CostEstimate(
        flops=tiles * 64 * BLK * BLK * HDIM, bytes_accessed=1 << 20, transcendentals=tiles * 16 * BLK * BLK
    )
    return pl.pallas_call(
        kernel,
        in_specs=[smem] * scalars + [vmem] * (len(operands) - scalars),
        out_specs=[vmem] * len(outputs),
        out_shape=outputs,
        cost_estimate=cost,
        compiler_params=pltpu.CompilerParams(vmem_limit_bytes=32 << 20),
    )(*operands)


def both(tile, bias, qc_own, qc_sib, kv_a, kv_b, state=()):
    return in_vmem(functools.partial(both_kernel, tile), 4, STATE * 2, bias, qc_own, qc_sib, kv_a, kv_b, *state)


def last_sib(*operands):
    outputs = [pltpu.VMEM((BLK, HALF), jnp.bfloat16), pltpu.VMEM((PAIRS, BLK), jnp.float32)]
    return in_vmem(sib_kernel, 1, outputs, *operands)


def last_own(*operands):
    outputs = [jax.ShapeDtypeStruct((BLK, 2 * HALF), jnp.bfloat16), jax.ShapeDtypeStruct((2 * PAIRS, BLK), jnp.float32)]
    return in_vmem(own_kernel, 1, outputs, *operands)


def rotations(groups, shards):
    onward = []
    for group in range(groups):
        for place in range(shards):
            chip, core = divmod(place, 2)
            there = chip + (1 if core == 1 else -1)
            target = there * 2 + core if 0 <= there < shards // 2 else chip * 2 + 1 - core
            onward.append((group * shards + place, group * shards + target))
    return onward, [(target, source) for source, target in onward]


def after(value, *others):
    return lax.optimization_barrier((value, *others))[0]


def local(queries, key_rows, value_rows, document_ids, link_lists, block_keep, out_gain, cotangent):
    groups, shards = lax.axis_size("dp"), lax.axis_size("seq")
    onward, backward = rotations(groups, shards)
    siblings = [(i, i ^ 1) for i in range(groups * shards)]
    move = lambda value, pairs: lax.ppermute(value, AXES, pairs)
    gain = out_gain.reshape(1, -1)

    kv_own, kv_send = split_heads(key_rows, value_rows)
    kv_sib = move(kv_send, siblings)
    r1 = move(kv_own, onward)
    r2 = move(kv_sib, backward)
    qc_own, qc_send = split_heads(queries, cotangent)
    qc_sib = move(qc_send, siblings)
    bias = masks(block_keep, document_ids, link_lists)

    state = both(0, bias, qc_own, qc_sib, kv_own, kv_sib)
    r3 = move(after(kv_own, r1, *state), backward)
    r4 = move(after(kv_sib, r2), onward)
    state = both(4, bias, qc_own, qc_sib, r1, r2, state)
    r5 = move(after(r1, r3, *state), onward)
    r6 = move(after(r2, r4), backward)
    state = both(8, bias, qc_own, qc_sib, r3, r4, state)
    att_sib, terms = last_sib(bias, qc_sib, r5, state[2], state[3], gain)
    back = move(att_sib, siblings)
    attended, terms = last_own(bias, qc_own, r6, state[0], state[1], gain, terms, back)
    pieces = lax.all_to_all(terms.reshape(groups * shards, -1), AXES, 0, 0, tiled=True)
    return attended, jnp.sum(pieces, axis=0)


def solution(mesh):
    placed = (
        P(AXES, None),
        P(AXES, None),
        P(AXES, None),
        P("dp", None),
        P("dp", None, None),
        P("dp", None, None),
        P(),
        P(AXES, None),
    )
    return jax.shard_map(local, mesh=mesh, in_specs=placed, out_specs=(P(AXES, None), P(AXES)), check_vma=False)
```

```python
import functools
import math

import jax
import jax.numpy as jnp
from jax import lax
from jax.experimental import pallas as pl
from jax.experimental.pallas import tpu as pltpu
from jax.sharding import PartitionSpec as P

HEADS = 32
HDIM = 64
REACH = 3
BLK = 128
HALF = HEADS * HDIM // 2
PAIRS = HALF // 128
NEGATIVE_FILL = -1e30
AXES = ("dp", "seq")


def split_kernel(key_ref, value_ref, query_ref, cotangent_ref, own_ref, send_ref, send_qc_ref, sems):
    core = lax.axis_index("seq") % 2
    mine = pl.ds(pl.multiple_of(core * HALF, HALF), HALF)
    others = pl.ds(pl.multiple_of((1 - core) * HALF, HALF), HALF)
    moves = [(key_ref, mine, own_ref, 0), (value_ref, mine, own_ref, 1)]
    moves += [(key_ref, others, send_ref, 0), (value_ref, others, send_ref, 1)]
    moves += [(query_ref, others, send_qc_ref, 0), (cotangent_ref, others, send_qc_ref, 1)]
    copies = []
    for at, (source, columns, target, part) in enumerate(moves):
        copies.append(pltpu.make_async_copy(source.at[:, columns], target.at[cols(part)], sems.at[at]))
    for copy in copies:
        copy.start()
    for copy in copies:
        copy.wait()


def split_heads(*arrays):
    shape = pltpu.VMEM((2 * BLK, HALF), jnp.bfloat16)
    return pl.pallas_call(
        split_kernel,
        in_specs=[pl.BlockSpec(memory_space=pl.ANY)] * 4,
        out_specs=[pl.BlockSpec(memory_space=pltpu.VMEM)] * 3,
        out_shape=[shape] * 3,
        scratch_shapes=[pltpu.SemaphoreType.DMA((6,))],
        cost_estimate=pl.CostEstimate(flops=0, bytes_accessed=3 << 20, transcendentals=0),
    )(*arrays)


OWN, SIB, R1, R2, R3, R4, R5, R6 = range(8)
TILES = (
    [(q, k) for q in (OWN, SIB) for k in (OWN, SIB)]
    + [(q, k) for q in (OWN, SIB) for k in (R1, R2)]
    + [(q, k) for q in (OWN, SIB) for k in (R3, R4)]
    + [(SIB, R5), (OWN, R6)]
)


def key_blocks():
    place = lax.axis_index("seq")
    chip, core = place // 2, place % 2
    toward = 1 - 2 * core
    ring = [(chip, core), (chip, 1 - core)]
    ring += [(chip + toward, core), (chip - toward, 1 - core), (chip - toward, core), (chip + toward, 1 - core)]
    ring += [(chip + 2 * toward, core), (chip - 2 * toward, 1 - core)]
    return [2 * at + side for at, side in ring]


def mask_kernel(keep_ref, docs_ref, links_ref, bias_ref):
    docs_in_pack = links_ref.shape[1]
    nblk = docs_ref.shape[1] // BLK
    blocks = key_blocks()
    target = lax.broadcasted_iota(jnp.int32, (docs_in_pack, docs_in_pack), 1)
    source = lax.broadcasted_iota(jnp.int32, (docs_in_pack, docs_in_pack), 0)
    links = links_ref[0]
    linked = target == links[:, 0:1]
    for at in range(1, links.shape[1]):
        linked = linked | (target == links[:, at : at + 1])
    table = jnp.where(source == target, 2.0, 0.0) + jnp.where(linked, 1.0, 0.0)
    table = table.astype(jnp.bfloat16)

    def one_hot(block):
        at = pl.multiple_of(jnp.clip(block, 0, nblk - 1) * BLK, BLK)
        row = docs_ref[:, pl.ds(at, BLK)]
        rows = lax.broadcasted_iota(jnp.int32, (docs_in_pack, BLK), 0)
        return jnp.where(rows == row, 1.0, 0.0).astype(jnp.bfloat16)

    hots = [one_hot(block) for block in blocks]
    related = [
        lax.dot_general(table, hots[q], (((0,), (0,)), ((), ())), preferred_element_type=jnp.float32).astype(jnp.bfloat16)
        for q in (OWN, SIB)
    ]
    key_at = lax.broadcasted_iota(jnp.int32, (BLK, BLK), 0)
    query_at = lax.broadcasted_iota(jnp.int32, (BLK, BLK), 1)
    apart = query_at - key_at
    for tile, (q, k) in enumerate(TILES):
        query_block, key_block = blocks[q], blocks[k]
        present = (key_block >= 0) & (key_block < nblk)
        kept = keep_ref[0, query_block, jnp.clip(key_block, 0, nblk - 1)] == 1
        least = jnp.where(present, jnp.where(kept, 0.5, 1.5), 9.0)
        relation = lax.dot_general(hots[k], related[q], (((0,), (0,)), ((), ())), preferred_element_type=jnp.float32)
        distance = apart + (query_block - key_block) * BLK
        allowed = (relation > least) & (jnp.abs(distance) <= REACH * BLK)
        bias_ref[tile * BLK : (tile + 1) * BLK] = jnp.where(allowed, 0.0, NEGATIVE_FILL)


def masks(keep, docs, links):
    return in_vmem(mask_kernel, 1, [pltpu.VMEM((len(TILES) * BLK, BLK), jnp.float32)], keep, docs, links, scalars=1)[0]


def absorb(queries, keys, values, biases, state):
    stacked = []
    for query in queries:
        low = lax.broadcasted_iota(jnp.int32, query.shape, 1) < HDIM
        scaled = query * jnp.bfloat16(1.0 / math.sqrt(HDIM))
        nothing = jnp.zeros_like(scaled)
        stacked += [jnp.where(low, scaled, nothing), jnp.where(low, nothing, scaled)]
    scores = lax.dot_general(
        keys, jnp.concatenate(stacked, axis=0), (((1,), (1,)), ((), ())), preferred_element_type=jnp.float32
    )
    scores = scores + jnp.concatenate([bias for bias in biases for _ in range(2)], axis=1)
    largest = jnp.max(scores, axis=0, keepdims=True)
    if state is not None:
        largest = jnp.maximum(state[0], largest)
    expo = jnp.exp(scores - largest)
    totals = jnp.sum(expo, axis=0, keepdims=True)
    sums = lax.dot_general(
        values, expo.astype(jnp.bfloat16), (((0,), (0,)), ((), ())), preferred_element_type=jnp.float32
    )
    folded = fold(sums[:HDIM], sums[HDIM:])
    if state is not None:
        shrink = jnp.exp(state[0] - largest)
        totals = totals + state[1] * shrink
        folded = folded + state[2] * spread(shrink)
    return largest, totals, folded


def fold(first, second):
    blocks = range(0, first.shape[1], 2 * BLK)
    pieces = [jnp.concatenate([first[:, at : at + BLK], second[:, at + BLK : at + 2 * BLK]], axis=0) for at in blocks]
    return jnp.concatenate(pieces, axis=1)


def spread(row):
    wide = jnp.broadcast_to(row, (HDIM, row.shape[1]))
    return fold(wide, wide)


def cols(at):
    return slice(at * BLK, (at + 1) * BLK)


def my_cols(at):
    core = lax.axis_index("seq") % 2
    return pl.ds(pl.multiple_of(core * HALF + at * BLK, BLK), BLK)


def put_state(rows_ref, sums_ref, at, state):
    rows_ref[at * 8 : at * 8 + 1] = state[0]
    rows_ref[at * 8 + 1 : at * 8 + 2] = state[1]
    sums_ref[cols(at)] = state[2]


def get_state(rows_ref, sums_ref, at, first=0, blocks=2):
    of_rows = slice(first * 2 * BLK, (first + blocks) * 2 * BLK)
    of_sums = slice(first * BLK, (first + blocks) * BLK)
    return rows_ref[at * 8 : at * 8 + 1, of_rows], rows_ref[at * 8 + 1 : at * 8 + 2, of_rows], sums_ref[cols(at), of_sums]


def both_kernel(tile, bias_ref, query_ref, qc_sib, kv_a, kv_b, *states):
    before, now = states[:-2], states[-2:]
    for at in range(PAIRS):
        at_cols = cols(at)
        keys = jnp.concatenate([kv_a[:BLK, at_cols], kv_b[:BLK, at_cols]], axis=0)
        values = jnp.concatenate([kv_a[BLK:, at_cols], kv_b[BLK:, at_cols]], axis=0)
        queries = [query_ref[:, my_cols(at)], qc_sib[:BLK, at_cols]]
        biases = [bias_ref[(tile + 2 * side) * BLK : (tile + 2 * side + 2) * BLK] for side in range(2)]
        state = get_state(*before, at) if before else None
        put_state(*now, at, absorb(queries, keys, values, biases, state))


def finish(state, gain, cotangent):
    mixed = jnp.transpose(state[2] / spread(state[1]))
    attended = (gain * mixed).astype(jnp.bfloat16)
    terms = jnp.sum(mixed * cotangent.astype(jnp.float32), axis=0, keepdims=True)
    return attended, terms


def last(tile, side, at, bias_ref, query, cotangent, kv, rows, sums, gain_ref):
    at_cols = cols(at)
    state = get_state(rows, sums, at, side, 1)
    state = absorb([query], kv[:BLK, at_cols], kv[BLK:, at_cols], [bias_ref[cols(tile)]], state)
    return finish(state, gain_ref[:, my_cols(at)], cotangent)


def sib_kernel(bias_ref, qc, kv, rows, sums, gain_ref, att_ref, terms_ref):
    for at in range(PAIRS):
        query, cotangent = qc[:BLK, cols(at)], qc[BLK:, cols(at)]
        att_ref[:, cols(at)], terms = last(12, 1, at, bias_ref, query, cotangent, kv, rows, sums, gain_ref)
        terms_ref[at : at + 1] = terms


def own_kernel(
    bias_ref, query_ref, cotangent_ref, kv, rows, sums, gain_ref, terms_in, out_ref, terms_ref, att, spread_terms, sems
):
    core = lax.axis_index("seq") % 2
    devices = terms_ref.shape[0] // (2 * PAIRS)
    copies = []

    def send(source, target):
        copies.append(pltpu.make_async_copy(source, target, sems.at[len(copies)]))
        copies[-1].start()

    half = PAIRS * devices
    here = pl.ds(pl.multiple_of((1 - core) * half, half), half)
    spread_terms[here] = jnp.zeros((half, BLK), jnp.float32)
    send(spread_terms.at[here], terms_ref.at[here])
    for at in range(PAIRS):
        query, cotangent = query_ref[:, my_cols(at)], cotangent_ref[:, my_cols(at)]
        att[:, cols(at)], terms = last(13, 0, at, bias_ref, query, cotangent, kv, rows, sums, gain_ref)
        send(att.at[:, cols(at)], out_ref.at[:, my_cols(at)])
        here = pl.ds(pl.multiple_of((core * PAIRS + at) * devices, devices), devices)
        spread_terms[here] = jnp.broadcast_to(terms + terms_in[at : at + 1], (devices, BLK))
        send(spread_terms.at[here], terms_ref.at[here])
    for copy in copies:
        copy.wait()


def fill_kernel(back_ref, out_in, out_ref, sem):
    core = lax.axis_index("seq") % 2
    there = pl.ds(pl.multiple_of((1 - core) * HALF, HALF), HALF)
    copy = pltpu.make_async_copy(back_ref, out_ref.at[:, there], sem)
    copy.start()
    copy.wait()


def fill_heads(back, out):
    return pl.pallas_call(
        fill_kernel,
        in_specs=[pl.BlockSpec(memory_space=pltpu.VMEM), pl.BlockSpec(memory_space=pl.ANY)],
        out_specs=pl.BlockSpec(memory_space=pl.ANY),
        out_shape=jax.ShapeDtypeStruct(out.shape, out.dtype),
        input_output_aliases={1: 0},
        scratch_shapes=[pltpu.SemaphoreType.DMA],
        cost_estimate=pl.CostEstimate(flops=0, bytes_accessed=1 << 20, transcendentals=0),
    )(back, out)


STATE = [pltpu.VMEM((PAIRS * 8, 4 * BLK), jnp.float32), pltpu.VMEM((PAIRS * BLK, 2 * BLK), jnp.float32)]


def in_vmem(kernel, tiles, outputs, *operands, scalars=0):
    vmem = pl.BlockSpec(memory_space=pltpu.VMEM)
    smem = pl.BlockSpec(memory_space=pltpu.SMEM)
    cost = pl.CostEstimate(
        flops=tiles * 64 * BLK * BLK * HDIM, bytes_accessed=1 << 20, transcendentals=tiles * 16 * BLK * BLK
    )
    return pl.pallas_call(
        kernel,
        in_specs=[smem] * scalars + [vmem] * (len(operands) - scalars),
        out_specs=[vmem] * len(outputs),
        out_shape=outputs,
        cost_estimate=cost,
        compiler_params=pltpu.CompilerParams(vmem_limit_bytes=8 << 20),
    )(*operands)


def both(tile, bias, queries, qc_sib, kv_a, kv_b, state=()):
    return in_vmem(functools.partial(both_kernel, tile), 4, STATE, bias, queries, qc_sib, kv_a, kv_b, *state)


def last_sib(*operands):
    outputs = [pltpu.VMEM((BLK, HALF), jnp.bfloat16), pltpu.VMEM((PAIRS, BLK), jnp.float32)]
    return in_vmem(sib_kernel, 1, outputs, *operands)


def last_own(devices, *operands):
    return pl.pallas_call(
        own_kernel,
        in_specs=[pl.BlockSpec(memory_space=pltpu.VMEM)] * len(operands),
        out_specs=[pl.BlockSpec(memory_space=pl.ANY)] * 2,
        out_shape=[
            jax.ShapeDtypeStruct((BLK, 2 * HALF), jnp.bfloat16),
            jax.ShapeDtypeStruct((devices, BLK), jnp.float32),
        ],
        scratch_shapes=[
            pltpu.VMEM((BLK, HALF), jnp.bfloat16),
            pltpu.VMEM((devices, BLK), jnp.float32),
            pltpu.SemaphoreType.DMA((1 + 2 * PAIRS,)),
        ],
        cost_estimate=pl.CostEstimate(flops=64 * BLK * BLK * HDIM, bytes_accessed=1 << 20, transcendentals=16 * BLK * BLK),
        compiler_params=pltpu.CompilerParams(vmem_limit_bytes=8 << 20),
    )(*operands)


def sum_kernel(pieces_ref, out_ref):
    mine = out_ref.shape[1]
    place = lax.axis_index("dp") * lax.axis_size("seq") + lax.axis_index("seq")
    total = jnp.sum(pieces_ref[...], axis=0, keepdims=True)
    at = lax.rem(place, BLK // mine) * mine
    out_ref[...] = pltpu.roll(total, lax.rem(BLK - at, BLK), 1)[:, :mine]


def rotations(groups, shards):
    onward = []
    for group in range(groups):
        for place in range(shards):
            chip, core = divmod(place, 2)
            there = chip + (1 if core == 1 else -1)
            target = there * 2 + core if 0 <= there < shards // 2 else chip * 2 + 1 - core
            onward.append((group * shards + place, group * shards + target))
    backward = [(target, source) for source, target in onward]
    crossing = lambda ring: [(at, to ^ 1 if to // 2 != at // 2 else at) for at, to in ring]
    return onward, backward, crossing(onward), crossing(backward)


def after(value, *others):
    return lax.optimization_barrier((value, *others))[0]


def local(queries, key_rows, value_rows, document_ids, link_lists, block_keep, out_gain, cotangent):
    groups, shards = lax.axis_size("dp"), lax.axis_size("seq")
    onward, backward, outward, inward = rotations(groups, shards)
    siblings = [(i, i ^ 1) for i in range(groups * shards)]
    move = lambda value, pairs: lax.ppermute(value, AXES, pairs)
    gain = out_gain.reshape(1, -1)

    kv_own, kv_send, qc_send = split_heads(key_rows, value_rows, queries, cotangent)
    r1 = move(kv_own, onward)
    r2 = move(kv_send, outward)
    kv_sib = move(kv_send, siblings)
    qc_sib = move(qc_send, siblings)
    bias = masks(block_keep, document_ids, link_lists)
    r3 = move(after(kv_own, qc_sib), backward)
    r4 = move(after(kv_send, qc_sib), inward)
    r5 = move(r1, onward)
    state = both(0, bias, queries, qc_sib, kv_own, kv_sib)
    r6 = move(after(r2, *state), backward)
    state = both(4, bias, queries, qc_sib, r1, r2, state)
    state = both(8, bias, queries, qc_sib, r3, r4, state)
    att_sib, terms = last_sib(bias, qc_sib, r5, *state, gain)
    back = move(att_sib, siblings)
    out, terms = last_own(groups * shards, bias, queries, cotangent, r6, *state, gain, terms)
    pieces = lax.all_to_all(terms.reshape(groups * shards, 1, BLK), AXES, 0, 0, tiled=True)
    attended = fill_heads(back, out)
    pieces = after(pieces, attended)
    mine = jax.ShapeDtypeStruct((1, 2 * HALF // (groups * shards)), jnp.float32)
    (gain_grad,) = in_vmem(sum_kernel, 0, [mine], pieces.reshape(groups * shards, BLK))
    return attended, gain_grad.reshape(-1)


def solution(mesh):
    placed = (
        P(AXES, None),
        P(AXES, None),
        P(AXES, None),
        P("dp", None),
        P("dp", None, None),
        P("dp", None, None),
        P(),
        P(AXES, None),
    )
    return jax.shard_map(local, mesh=mesh, in_specs=placed, out_specs=(P(AXES, None), P(AXES)), check_vma=False)
```

```python
import functools
import math

import jax
import jax.numpy as jnp
from jax import lax
from jax.experimental import pallas as pl
from jax.experimental.pallas import tpu as pltpu
from jax.sharding import PartitionSpec as P

HEADS = 32
HDIM = 64
REACH = 3
BLK = 128
HALF = HEADS * HDIM // 2
PAIRS = HALF // 128
NEGATIVE_FILL = -1e30
AXES = ("dp", "seq")


def split_kernel(sides, count, *refs):
    sources, targets, sems = refs[:count], refs[count:-1], refs[-1]
    core = lax.axis_index("seq") % 2
    copies = []
    for side, target in zip(sides, targets):
        columns = pl.ds(pl.multiple_of((core if side == 0 else 1 - core) * HALF, HALF), HALF)
        for part, source in enumerate(sources):
            copy = pltpu.make_async_copy(source.at[:, columns], target.at[cols(part)], sems.at[len(copies)])
            copies.append(copy)
    for copy in copies:
        copy.start()
    for copy in copies:
        copy.wait()


def split_heads(sides, *arrays):
    count = len(sides)
    return pl.pallas_call(
        functools.partial(split_kernel, sides, 2),
        in_specs=[pl.BlockSpec(memory_space=pl.ANY)] * 2,
        out_specs=[pl.BlockSpec(memory_space=pltpu.VMEM)] * count,
        out_shape=[pltpu.VMEM((2 * BLK, HALF), jnp.bfloat16)] * count,
        scratch_shapes=[pltpu.SemaphoreType.DMA((2 * count,))],
        cost_estimate=pl.CostEstimate(flops=0, bytes_accessed=count << 19, transcendentals=0),
    )(*arrays)


OWN, SIB, R1, R2, R3, R4, R5, R6 = range(8)
TILES = (
    [(q, k) for q in (OWN, SIB) for k in (OWN, SIB)]
    + [(q, k) for q in (OWN, SIB) for k in (R1, R2)]
    + [(q, k) for q in (OWN, SIB) for k in (R3, R4)]
    + [(SIB, R5), (OWN, R6)]
)


def key_blocks():
    place = lax.axis_index("seq")
    chip, core = place // 2, place % 2
    toward = 1 - 2 * core
    ring = [(chip, core), (chip, 1 - core)]
    ring += [(chip + toward, core), (chip - toward, 1 - core), (chip - toward, core), (chip + toward, 1 - core)]
    ring += [(chip + 2 * toward, core), (chip - 2 * toward, 1 - core)]
    return [2 * at + side for at, side in ring]


def mask_kernel(keep_ref, docs_ref, links_ref, bias_ref):
    docs_in_pack = links_ref.shape[1]
    nblk = docs_ref.shape[1] // BLK
    blocks = key_blocks()
    target = lax.broadcasted_iota(jnp.int32, (docs_in_pack, docs_in_pack), 1)
    source = lax.broadcasted_iota(jnp.int32, (docs_in_pack, docs_in_pack), 0)
    links = links_ref[0]
    linked = target == links[:, 0:1]
    for at in range(1, links.shape[1]):
        linked = linked | (target == links[:, at : at + 1])
    table = jnp.where(source == target, 2.0, 0.0) + jnp.where(linked, 1.0, 0.0)
    table = table.astype(jnp.bfloat16)

    def one_hot(block):
        at = pl.multiple_of(jnp.clip(block, 0, nblk - 1) * BLK, BLK)
        row = docs_ref[:, pl.ds(at, BLK)]
        rows = lax.broadcasted_iota(jnp.int32, (docs_in_pack, BLK), 0)
        return jnp.where(rows == row, 1.0, 0.0).astype(jnp.bfloat16)

    hots = [one_hot(block) for block in blocks]
    related = [
        lax.dot_general(table, hots[q], (((0,), (0,)), ((), ())), preferred_element_type=jnp.float32).astype(jnp.bfloat16)
        for q in (OWN, SIB)
    ]
    key_at = lax.broadcasted_iota(jnp.int32, (BLK, BLK), 0)
    query_at = lax.broadcasted_iota(jnp.int32, (BLK, BLK), 1)
    apart = query_at - key_at
    for tile, (q, k) in enumerate(TILES):
        query_block, key_block = blocks[q], blocks[k]
        present = (key_block >= 0) & (key_block < nblk)
        kept = keep_ref[0, query_block, jnp.clip(key_block, 0, nblk - 1)] == 1
        least = jnp.where(present, jnp.where(kept, 0.5, 1.5), 9.0)
        relation = lax.dot_general(hots[k], related[q], (((0,), (0,)), ((), ())), preferred_element_type=jnp.float32)
        distance = apart + (query_block - key_block) * BLK
        allowed = (relation > least) & (jnp.abs(distance) <= REACH * BLK)
        bias_ref[tile * BLK : (tile + 1) * BLK] = jnp.where(allowed, 0.0, NEGATIVE_FILL)


def masks(keep, docs, links):
    return in_vmem(mask_kernel, 1, [pltpu.VMEM((len(TILES) * BLK, BLK), jnp.float32)], keep, docs, links, scalars=1)[0]


def absorb(queries, keys, values, biases, state):
    stacked = []
    for query in queries:
        low = lax.broadcasted_iota(jnp.int32, query.shape, 1) < HDIM
        scaled = query * jnp.bfloat16(1.0 / math.sqrt(HDIM))
        nothing = jnp.zeros_like(scaled)
        stacked += [jnp.where(low, scaled, nothing), jnp.where(low, nothing, scaled)]
    scores = lax.dot_general(
        keys, jnp.concatenate(stacked, axis=0), (((1,), (1,)), ((), ())), preferred_element_type=jnp.float32
    )
    scores = scores + jnp.concatenate([bias for bias in biases for _ in range(2)], axis=1)
    largest = jnp.max(scores, axis=0, keepdims=True)
    if state is not None:
        largest = jnp.maximum(state[0], largest)
    expo = jnp.exp(scores - largest)
    totals = jnp.sum(expo, axis=0, keepdims=True)
    sums = lax.dot_general(
        values, expo.astype(jnp.bfloat16), (((0,), (0,)), ((), ())), preferred_element_type=jnp.float32
    )
    folded = fold(sums[:HDIM], sums[HDIM:])
    if state is not None:
        shrink = jnp.exp(state[0] - largest)
        totals = totals + state[1] * shrink
        folded = folded + state[2] * spread(shrink)
    return largest, totals, folded


def fold(first, second):
    blocks = range(0, first.shape[1], 2 * BLK)
    pieces = [jnp.concatenate([first[:, at : at + BLK], second[:, at + BLK : at + 2 * BLK]], axis=0) for at in blocks]
    return jnp.concatenate(pieces, axis=1)


def spread(row):
    wide = jnp.broadcast_to(row, (HDIM, row.shape[1]))
    return fold(wide, wide)


def cols(at):
    return slice(at * BLK, (at + 1) * BLK)


def my_cols(at):
    core = lax.axis_index("seq") % 2
    return pl.ds(pl.multiple_of(core * HALF + at * BLK, BLK), BLK)


def put_state(rows_ref, sums_ref, at, state):
    rows_ref[at * 8 : at * 8 + 1] = state[0]
    rows_ref[at * 8 + 1 : at * 8 + 2] = state[1]
    sums_ref[cols(at)] = state[2]


def get_state(rows_ref, sums_ref, at, first=0, blocks=2):
    of_rows = slice(first * 2 * BLK, (first + blocks) * 2 * BLK)
    of_sums = slice(first * BLK, (first + blocks) * BLK)
    return rows_ref[at * 8 : at * 8 + 1, of_rows], rows_ref[at * 8 + 1 : at * 8 + 2, of_rows], sums_ref[cols(at), of_sums]


def both_kernel(tile, count, bias_ref, query_ref, qc_sib, *refs):
    blocks, before, now = refs[:count], refs[count:-2], refs[-2:]
    for at in range(PAIRS):
        at_cols = cols(at)
        keys = jnp.concatenate([block[:BLK, at_cols] for block in blocks], axis=0)
        values = jnp.concatenate([block[BLK:, at_cols] for block in blocks], axis=0)
        queries = [query_ref[:, my_cols(at)], qc_sib[:BLK, at_cols]]
        biases = [bias_ref[(tile + 2 * side) * BLK : (tile + 2 * side + count) * BLK] for side in range(2)]
        state = get_state(*before, at) if before else None
        put_state(*now, at, absorb(queries, keys, values, biases, state))


def finish(state, gain, cotangent):
    mixed = jnp.transpose(state[2] / spread(state[1]))
    attended = (gain * mixed).astype(jnp.bfloat16)
    terms = jnp.sum(mixed * cotangent.astype(jnp.float32), axis=0, keepdims=True)
    return attended, terms


def last(tile, side, at, bias_ref, query, cotangent, kv, rows, sums, gain_ref):
    at_cols = cols(at)
    state = get_state(rows, sums, at, side, 1)
    state = absorb([query], kv[:BLK, at_cols], kv[BLK:, at_cols], [bias_ref[cols(tile)]], state)
    return finish(state, gain_ref[:, my_cols(at)], cotangent)


def sib_kernel(bias_ref, qc, kv, rows, sums, gain_ref, att_ref, terms_ref):
    for at in range(PAIRS):
        query, cotangent = qc[:BLK, cols(at)], qc[BLK:, cols(at)]
        att_ref[:, cols(at)], terms = last(12, 1, at, bias_ref, query, cotangent, kv, rows, sums, gain_ref)
        terms_ref[at : at + 1] = terms


def own_kernel(
    bias_ref, query_ref, cotangent_ref, kv, rows, sums, gain_ref, terms_in, out_ref, terms_ref, att, spread_terms, sems
):
    core = lax.axis_index("seq") % 2
    devices = terms_ref.shape[0] // (2 * PAIRS)
    copies = []

    def send(source, target):
        copies.append(pltpu.make_async_copy(source, target, sems.at[len(copies)]))
        copies[-1].start()

    half = PAIRS * devices
    here = pl.ds(pl.multiple_of((1 - core) * half, half), half)
    spread_terms[here] = jnp.zeros((half, BLK), jnp.float32)
    send(spread_terms.at[here], terms_ref.at[here])
    for at in range(PAIRS):
        query, cotangent = query_ref[:, my_cols(at)], cotangent_ref[:, my_cols(at)]
        att[:, cols(at)], terms = last(13, 0, at, bias_ref, query, cotangent, kv, rows, sums, gain_ref)
        send(att.at[:, cols(at)], out_ref.at[:, my_cols(at)])
        here = pl.ds(pl.multiple_of((core * PAIRS + at) * devices, devices), devices)
        spread_terms[here] = jnp.broadcast_to(terms + terms_in[at : at + 1], (devices, BLK))
        send(spread_terms.at[here], terms_ref.at[here])
    for copy in copies:
        copy.wait()


def fill_kernel(back_ref, out_in, out_ref, sem):
    core = lax.axis_index("seq") % 2
    there = pl.ds(pl.multiple_of((1 - core) * HALF, HALF), HALF)
    copy = pltpu.make_async_copy(back_ref, out_ref.at[:, there], sem)
    copy.start()
    copy.wait()


def fill_heads(back, out):
    return pl.pallas_call(
        fill_kernel,
        in_specs=[pl.BlockSpec(memory_space=pltpu.VMEM), pl.BlockSpec(memory_space=pl.ANY)],
        out_specs=pl.BlockSpec(memory_space=pl.ANY),
        out_shape=jax.ShapeDtypeStruct(out.shape, out.dtype),
        input_output_aliases={1: 0},
        scratch_shapes=[pltpu.SemaphoreType.DMA],
        cost_estimate=pl.CostEstimate(flops=0, bytes_accessed=1 << 20, transcendentals=0),
    )(back, out)


STATE = [pltpu.VMEM((PAIRS * 8, 4 * BLK), jnp.float32), pltpu.VMEM((PAIRS * BLK, 2 * BLK), jnp.float32)]


def in_vmem(kernel, tiles, outputs, *operands, scalars=0):
    vmem = pl.BlockSpec(memory_space=pltpu.VMEM)
    smem = pl.BlockSpec(memory_space=pltpu.SMEM)
    cost = pl.CostEstimate(
        flops=tiles * 64 * BLK * BLK * HDIM, bytes_accessed=1 << 20, transcendentals=tiles * 16 * BLK * BLK
    )
    return pl.pallas_call(
        kernel,
        in_specs=[smem] * scalars + [vmem] * (len(operands) - scalars),
        out_specs=[vmem] * len(outputs),
        out_shape=outputs,
        cost_estimate=cost,
        compiler_params=pltpu.CompilerParams(vmem_limit_bytes=8 << 20),
    )(*operands)


def both(tile, bias, queries, qc_sib, blocks, state=()):
    kernel = functools.partial(both_kernel, tile, len(blocks))
    return in_vmem(kernel, 2 * len(blocks), STATE, bias, queries, qc_sib, *blocks, *state)


def last_sib(*operands):
    outputs = [pltpu.VMEM((BLK, HALF), jnp.bfloat16), pltpu.VMEM((PAIRS, BLK), jnp.float32)]
    return in_vmem(sib_kernel, 1, outputs, *operands)


def last_own(devices, *operands):
    return pl.pallas_call(
        own_kernel,
        in_specs=[pl.BlockSpec(memory_space=pltpu.VMEM)] * len(operands),
        out_specs=[pl.BlockSpec(memory_space=pl.ANY)] * 2,
        out_shape=[
            jax.ShapeDtypeStruct((BLK, 2 * HALF), jnp.bfloat16),
            jax.ShapeDtypeStruct((devices, BLK), jnp.float32),
        ],
        scratch_shapes=[
            pltpu.VMEM((BLK, HALF), jnp.bfloat16),
            pltpu.VMEM((devices, BLK), jnp.float32),
            pltpu.SemaphoreType.DMA((1 + 2 * PAIRS,)),
        ],
        cost_estimate=pl.CostEstimate(flops=64 * BLK * BLK * HDIM, bytes_accessed=1 << 20, transcendentals=16 * BLK * BLK),
        compiler_params=pltpu.CompilerParams(vmem_limit_bytes=8 << 20),
    )(*operands)


def sum_kernel(pieces_ref, out_ref):
    mine = out_ref.shape[1]
    place = lax.axis_index("dp") * lax.axis_size("seq") + lax.axis_index("seq")
    total = jnp.sum(pieces_ref[...], axis=0, keepdims=True)
    at = lax.rem(place, BLK // mine) * mine
    out_ref[...] = pltpu.roll(total, lax.rem(BLK - at, BLK), 1)[:, :mine]


def rotations(groups, shards):
    onward = []
    for group in range(groups):
        for place in range(shards):
            chip, core = divmod(place, 2)
            there = chip + (1 if core == 1 else -1)
            target = there * 2 + core if 0 <= there < shards // 2 else chip * 2 + 1 - core
            onward.append((group * shards + place, group * shards + target))
    backward = [(target, source) for source, target in onward]
    crossing = lambda ring: [(at, to ^ 1 if to // 2 != at // 2 else at) for at, to in ring]
    return onward, backward, crossing(onward), crossing(backward)


def after(value, *others):
    return lax.optimization_barrier((value, *others))[0]


def local(queries, key_rows, value_rows, document_ids, link_lists, block_keep, out_gain, cotangent):
    groups, shards = lax.axis_size("dp"), lax.axis_size("seq")
    onward, backward, outward, inward = rotations(groups, shards)
    siblings = [(i, i ^ 1) for i in range(groups * shards)]
    move = lambda value, pairs: lax.ppermute(value, AXES, pairs)
    gain = out_gain.reshape(1, -1)

    kv_own, kv_send = split_heads((0, 1), key_rows, value_rows)
    r1 = move(kv_own, onward)
    r2 = move(kv_send, outward)
    kv_sib = move(kv_send, siblings)
    (qc_send,) = split_heads((1,), after(queries, kv_sib), cotangent)
    qc_sib = move(qc_send, siblings)
    r3 = move(after(kv_own, qc_sib), backward)
    r4 = move(after(kv_send, qc_sib), inward)
    r5 = move(r1, onward)
    bias = masks(block_keep, after(document_ids, kv_sib), link_lists)
    state = both(0, bias, queries, qc_sib, (kv_own, kv_sib))
    r6 = move(after(r2, *state), backward)
    state = both(4, bias, queries, qc_sib, (r1, r2), state)
    state = both(8, bias, queries, qc_sib, (r3,), state)
    state = both(9, bias, queries, qc_sib, (r4,), state)
    att_sib, terms = last_sib(bias, qc_sib, r5, *state, gain)
    back = move(att_sib, siblings)
    out, terms = last_own(groups * shards, bias, queries, cotangent, r6, *state, gain, terms)
    pieces = lax.all_to_all(terms.reshape(groups * shards, 1, BLK), AXES, 0, 0, tiled=True)
    attended = fill_heads(back, out)
    pieces = after(pieces, attended)
    mine = jax.ShapeDtypeStruct((1, 2 * HALF // (groups * shards)), jnp.float32)
    (gain_grad,) = in_vmem(sum_kernel, 0, [mine], pieces.reshape(groups * shards, BLK))
    return attended, gain_grad.reshape(-1)


def solution(mesh):
    placed = (
        P(AXES, None),
        P(AXES, None),
        P(AXES, None),
        P("dp", None),
        P("dp", None, None),
        P("dp", None, None),
        P(),
        P(AXES, None),
    )
    return jax.shard_map(local, mesh=mesh, in_specs=placed, out_specs=(P(AXES, None), P(AXES)), check_vma=False)
```

```python
import functools
import math

import jax
import jax.numpy as jnp
from jax import lax
from jax.experimental import pallas as pl
from jax.experimental.pallas import tpu as pltpu
from jax.sharding import PartitionSpec as P

HEADS = 32
HDIM = 64
REACH = 3
BLK = 128
HALF = HEADS * HDIM // 2
PAIRS = HALF // 128
SENT_AFTER = (3, 6, 8)
NEGATIVE_FILL = -1e30
AXES = ("dp", "seq")


def split_kernel(sides, count, *refs):
    sources, targets, sems = refs[:count], refs[count:-1], refs[-1]
    core = lax.axis_index("seq") % 2
    copies = []
    for side, target in zip(sides, targets):
        columns = pl.ds(pl.multiple_of((core if side == 0 else 1 - core) * HALF, HALF), HALF)
        for part, source in enumerate(sources):
            copy = pltpu.make_async_copy(source.at[:, columns], target.at[cols(part)], sems.at[len(copies)])
            copies.append(copy)
    for copy in copies:
        copy.start()
    for copy in copies:
        copy.wait()


def split_heads(sides, *arrays):
    count = len(sides)
    return pl.pallas_call(
        functools.partial(split_kernel, sides, 2),
        in_specs=[pl.BlockSpec(memory_space=pl.ANY)] * 2,
        out_specs=[pl.BlockSpec(memory_space=pltpu.VMEM)] * count,
        out_shape=[pltpu.VMEM((2 * BLK, HALF), jnp.bfloat16)] * count,
        scratch_shapes=[pltpu.SemaphoreType.DMA((2 * count,))],
        cost_estimate=pl.CostEstimate(flops=0, bytes_accessed=count << 19, transcendentals=0),
    )(*arrays)


OWN, SIB, R1, R2, R3, R4, R5, R6 = range(8)
TILES = (
    [(q, k) for q in (OWN, SIB) for k in (OWN, SIB)]
    + [(q, k) for q in (OWN, SIB) for k in (R1, R2)]
    + [(q, k) for q in (OWN, SIB) for k in (R3, R4)]
    + [(SIB, R5), (OWN, R6)]
)


def key_blocks():
    place = lax.axis_index("seq")
    chip, core = place // 2, place % 2
    toward = 1 - 2 * core
    ring = [(chip, core), (chip, 1 - core)]
    ring += [(chip + toward, core), (chip - toward, 1 - core), (chip - toward, core), (chip + toward, 1 - core)]
    ring += [(chip + 2 * toward, core), (chip - 2 * toward, 1 - core)]
    return [2 * at + side for at, side in ring]


def mask_kernel(keep_ref, docs_ref, links_ref, bias_ref):
    docs_in_pack = links_ref.shape[1]
    nblk = docs_ref.shape[1] // BLK
    blocks = key_blocks()
    target = lax.broadcasted_iota(jnp.int32, (docs_in_pack, docs_in_pack), 1)
    source = lax.broadcasted_iota(jnp.int32, (docs_in_pack, docs_in_pack), 0)
    links = links_ref[0]
    linked = target == links[:, 0:1]
    for at in range(1, links.shape[1]):
        linked = linked | (target == links[:, at : at + 1])
    table = jnp.where(source == target, 2.0, 0.0) + jnp.where(linked, 1.0, 0.0)
    table = table.astype(jnp.bfloat16)

    def one_hot(block):
        at = pl.multiple_of(jnp.clip(block, 0, nblk - 1) * BLK, BLK)
        row = docs_ref[:, pl.ds(at, BLK)]
        rows = lax.broadcasted_iota(jnp.int32, (docs_in_pack, BLK), 0)
        return jnp.where(rows == row, 1.0, 0.0).astype(jnp.bfloat16)

    hots = [one_hot(block) for block in blocks]
    related = [
        lax.dot_general(table, hots[q], (((0,), (0,)), ((), ())), preferred_element_type=jnp.float32).astype(jnp.bfloat16)
        for q in (OWN, SIB)
    ]
    key_at = lax.broadcasted_iota(jnp.int32, (BLK, BLK), 0)
    query_at = lax.broadcasted_iota(jnp.int32, (BLK, BLK), 1)
    apart = query_at - key_at
    for tile, (q, k) in enumerate(TILES):
        query_block, key_block = blocks[q], blocks[k]
        present = (key_block >= 0) & (key_block < nblk)
        kept = keep_ref[0, query_block, jnp.clip(key_block, 0, nblk - 1)] == 1
        least = jnp.where(present, jnp.where(kept, 0.5, 1.5), 9.0)
        relation = lax.dot_general(hots[k], related[q], (((0,), (0,)), ((), ())), preferred_element_type=jnp.float32)
        distance = apart + (query_block - key_block) * BLK
        allowed = (relation > least) & (jnp.abs(distance) <= REACH * BLK)
        bias_ref[tile * BLK : (tile + 1) * BLK] = jnp.where(allowed, 0.0, NEGATIVE_FILL)


def masks(keep, docs, links):
    return in_vmem(mask_kernel, 1, [pltpu.VMEM((len(TILES) * BLK, BLK), jnp.float32)], keep, docs, links, scalars=1)[0]


def absorb(queries, keys, values, biases, state):
    stacked = []
    for query in queries:
        low = lax.broadcasted_iota(jnp.int32, query.shape, 1) < HDIM
        scaled = query * jnp.bfloat16(1.0 / math.sqrt(HDIM))
        nothing = jnp.zeros_like(scaled)
        stacked += [jnp.where(low, scaled, nothing), jnp.where(low, nothing, scaled)]
    scores = lax.dot_general(
        keys, jnp.concatenate(stacked, axis=0), (((1,), (1,)), ((), ())), preferred_element_type=jnp.float32
    )
    scores = scores + jnp.concatenate([bias for bias in biases for _ in range(2)], axis=1)
    largest = jnp.max(scores, axis=0, keepdims=True)
    if state is not None:
        largest = jnp.maximum(state[0], largest)
    expo = jnp.exp(scores - largest)
    totals = jnp.sum(expo, axis=0, keepdims=True)
    sums = lax.dot_general(
        values, expo.astype(jnp.bfloat16), (((0,), (0,)), ((), ())), preferred_element_type=jnp.float32
    )
    folded = fold(sums[:HDIM], sums[HDIM:])
    if state is not None:
        shrink = jnp.exp(state[0] - largest)
        totals = totals + state[1] * shrink
        folded = folded + state[2] * spread(shrink)
    return largest, totals, folded


def fold(first, second):
    blocks = range(0, first.shape[1], 2 * BLK)
    pieces = [jnp.concatenate([first[:, at : at + BLK], second[:, at + BLK : at + 2 * BLK]], axis=0) for at in blocks]
    return jnp.concatenate(pieces, axis=1)


def spread(row):
    wide = jnp.broadcast_to(row, (HDIM, row.shape[1]))
    return fold(wide, wide)


def cols(at):
    return slice(at * BLK, (at + 1) * BLK)


def my_cols(at):
    core = lax.axis_index("seq") % 2
    return pl.ds(pl.multiple_of(core * HALF + at * BLK, BLK), BLK)


def put_state(rows_ref, sums_ref, at, state):
    rows_ref[at * 8 : at * 8 + 1] = state[0]
    rows_ref[at * 8 + 1 : at * 8 + 2] = state[1]
    sums_ref[cols(at)] = state[2]


def get_state(rows_ref, sums_ref, at, first=0, blocks=2):
    of_rows = slice(first * 2 * BLK, (first + blocks) * 2 * BLK)
    of_sums = slice(first * BLK, (first + blocks) * BLK)
    return rows_ref[at * 8 : at * 8 + 1, of_rows], rows_ref[at * 8 + 1 : at * 8 + 2, of_rows], sums_ref[cols(at), of_sums]


def both_kernel(tile, count, bias_ref, query_ref, qc_sib, *refs):
    blocks, before, now = refs[:count], refs[count:-2], refs[-2:]
    for at in range(PAIRS):
        at_cols = cols(at)
        keys = jnp.concatenate([block[:BLK, at_cols] for block in blocks], axis=0)
        values = jnp.concatenate([block[BLK:, at_cols] for block in blocks], axis=0)
        queries = [query_ref[:, my_cols(at)], qc_sib[:BLK, at_cols]]
        biases = [bias_ref[(tile + 2 * side) * BLK : (tile + 2 * side + count) * BLK] for side in range(2)]
        state = get_state(*before, at) if before else None
        put_state(*now, at, absorb(queries, keys, values, biases, state))


def finish(state, gain, cotangent):
    mixed = jnp.transpose(state[2] * spread(1.0 / state[1]))
    attended = (gain * mixed).astype(jnp.bfloat16)
    terms = jnp.sum(mixed * cotangent.astype(jnp.float32), axis=0, keepdims=True)
    return attended, terms


def last(tile, side, at, bias_ref, query, cotangent, kv, rows, sums, gain_ref):
    at_cols = cols(at)
    state = get_state(rows, sums, at, side, 1)
    state = absorb([query], kv[:BLK, at_cols], kv[BLK:, at_cols], [bias_ref[cols(tile)]], state)
    return finish(state, gain_ref[:, my_cols(at)], cotangent)


def sib_kernel(bias_ref, qc, kv, rows, sums, gain_ref, att_ref, terms_ref):
    for at in range(PAIRS):
        query, cotangent = qc[:BLK, cols(at)], qc[BLK:, cols(at)]
        att_ref[:, cols(at)], terms = last(12, 1, at, bias_ref, query, cotangent, kv, rows, sums, gain_ref)
        terms_ref[at : at + 1] = terms


def own_kernel(
    bias_ref, query_ref, cotangent_ref, kv, rows, sums, gain_ref, terms_in, out_ref, terms_ref, att, spread_terms, sems
):
    core = lax.axis_index("seq") % 2
    devices = terms_ref.shape[0] // (2 * PAIRS)
    copies = []

    def send(source, target):
        copies.append(pltpu.make_async_copy(source, target, sems.at[len(copies)]))
        copies[-1].start()

    half = PAIRS * devices
    there = pl.ds(pl.multiple_of((1 - core) * half, half), half)
    spread_terms[there] = jnp.zeros((half, BLK), jnp.float32)
    send(spread_terms.at[there], terms_ref.at[there])
    sent = 0
    for at in range(PAIRS):
        query, cotangent = query_ref[:, my_cols(at)], cotangent_ref[:, my_cols(at)]
        att[:, cols(at)], terms = last(13, 0, at, bias_ref, query, cotangent, kv, rows, sums, gain_ref)
        here = pl.ds(pl.multiple_of((core * PAIRS + at) * devices, devices), devices)
        spread_terms[here] = jnp.broadcast_to(terms + terms_in[at : at + 1], (devices, BLK))
        if at + 1 in SENT_AFTER:
            width = (at + 1 - sent) * BLK
            columns = pl.ds(pl.multiple_of(core * HALF + sent * BLK, BLK), width)
            send(att.at[:, sent * BLK : (at + 1) * BLK], out_ref.at[:, columns])
            place = (core * PAIRS + sent) * devices
            here = pl.ds(pl.multiple_of(place, devices), (at + 1 - sent) * devices)
            send(spread_terms.at[here], terms_ref.at[here])
            sent = at + 1
    for copy in copies:
        copy.wait()


def fill_kernel(back_ref, out_in, out_ref, sem):
    core = lax.axis_index("seq") % 2
    there = pl.ds(pl.multiple_of((1 - core) * HALF, HALF), HALF)
    copy = pltpu.make_async_copy(back_ref, out_ref.at[:, there], sem)
    copy.start()
    copy.wait()


def fill_heads(back, out):
    return pl.pallas_call(
        fill_kernel,
        in_specs=[pl.BlockSpec(memory_space=pltpu.VMEM), pl.BlockSpec(memory_space=pl.ANY)],
        out_specs=pl.BlockSpec(memory_space=pl.ANY),
        out_shape=jax.ShapeDtypeStruct(out.shape, out.dtype),
        input_output_aliases={1: 0},
        scratch_shapes=[pltpu.SemaphoreType.DMA],
        cost_estimate=pl.CostEstimate(flops=0, bytes_accessed=1 << 20, transcendentals=0),
    )(back, out)


STATE = [pltpu.VMEM((PAIRS * 8, 4 * BLK), jnp.float32), pltpu.VMEM((PAIRS * BLK, 2 * BLK), jnp.float32)]


def in_vmem(kernel, tiles, outputs, *operands, scalars=0):
    vmem = pl.BlockSpec(memory_space=pltpu.VMEM)
    smem = pl.BlockSpec(memory_space=pltpu.SMEM)
    cost = pl.CostEstimate(
        flops=tiles * 64 * BLK * BLK * HDIM, bytes_accessed=1 << 20, transcendentals=tiles * 16 * BLK * BLK
    )
    return pl.pallas_call(
        kernel,
        in_specs=[smem] * scalars + [vmem] * (len(operands) - scalars),
        out_specs=[vmem] * len(outputs),
        out_shape=outputs,
        cost_estimate=cost,
        compiler_params=pltpu.CompilerParams(vmem_limit_bytes=8 << 20),
    )(*operands)


def both(tile, bias, queries, qc_sib, blocks, state=()):
    kernel = functools.partial(both_kernel, tile, len(blocks))
    return in_vmem(kernel, 2 * len(blocks), STATE, bias, queries, qc_sib, *blocks, *state)


def last_sib(*operands):
    outputs = [pltpu.VMEM((BLK, HALF), jnp.bfloat16), pltpu.VMEM((PAIRS, BLK), jnp.float32)]
    return in_vmem(sib_kernel, 1, outputs, *operands)


def last_own(devices, *operands):
    return pl.pallas_call(
        own_kernel,
        in_specs=[pl.BlockSpec(memory_space=pltpu.VMEM)] * len(operands),
        out_specs=[pl.BlockSpec(memory_space=pl.ANY)] * 2,
        out_shape=[
            jax.ShapeDtypeStruct((BLK, 2 * HALF), jnp.bfloat16),
            jax.ShapeDtypeStruct((devices, BLK), jnp.float32),
        ],
        scratch_shapes=[
            pltpu.VMEM((BLK, HALF), jnp.bfloat16),
            pltpu.VMEM((devices, BLK), jnp.float32),
            pltpu.SemaphoreType.DMA((1 + 2 * len(SENT_AFTER),)),
        ],
        cost_estimate=pl.CostEstimate(flops=64 * BLK * BLK * HDIM, bytes_accessed=1 << 20, transcendentals=16 * BLK * BLK),
        compiler_params=pltpu.CompilerParams(vmem_limit_bytes=8 << 20),
    )(*operands)


def sum_kernel(pieces_ref, out_ref):
    mine = out_ref.shape[1]
    place = lax.axis_index("dp") * lax.axis_size("seq") + lax.axis_index("seq")
    total = jnp.sum(pieces_ref[...], axis=0, keepdims=True)
    at = lax.rem(place, BLK // mine) * mine
    out_ref[...] = pltpu.roll(total, lax.rem(BLK - at, BLK), 1)[:, :mine]


def rotations(groups, shards):
    onward = []
    for group in range(groups):
        for place in range(shards):
            chip, core = divmod(place, 2)
            there = chip + (1 if core == 1 else -1)
            target = there * 2 + core if 0 <= there < shards // 2 else chip * 2 + 1 - core
            onward.append((group * shards + place, group * shards + target))
    backward = [(target, source) for source, target in onward]
    crossing = lambda ring: [(at, to ^ 1 if to // 2 != at // 2 else at) for at, to in ring]
    return onward, backward, crossing(onward), crossing(backward)


def after(value, *others):
    return lax.optimization_barrier((value, *others))[0]


def local(queries, key_rows, value_rows, document_ids, link_lists, block_keep, out_gain, cotangent):
    groups, shards = lax.axis_size("dp"), lax.axis_size("seq")
    onward, backward, outward, inward = rotations(groups, shards)
    siblings = [(i, i ^ 1) for i in range(groups * shards)]
    move = lambda value, pairs: lax.ppermute(value, AXES, pairs)
    gain = out_gain.reshape(1, -1)

    kv_own, kv_send = split_heads((0, 1), key_rows, value_rows)
    r1 = move(kv_own, onward)
    r2 = move(kv_send, outward)
    kv_sib = move(kv_send, siblings)
    (qc_send,) = split_heads((1,), after(queries, kv_sib), cotangent)
    qc_sib = move(qc_send, siblings)
    r3 = move(after(kv_own, qc_sib), backward)
    r4 = move(after(kv_send, qc_sib), inward)
    r5 = move(r1, onward)
    bias = masks(block_keep, after(document_ids, kv_sib), link_lists)
    state = both(0, bias, queries, qc_sib, (kv_own, kv_sib))
    r6 = move(after(r2, *state), backward)
    state = both(4, bias, queries, qc_sib, (r1, r2), state)
    state = both(8, bias, queries, qc_sib, (r3,), state)
    state = both(9, bias, queries, qc_sib, (r4,), state)
    att_sib, terms = last_sib(bias, qc_sib, r5, *state, gain)
    back = move(att_sib, siblings)
    out, terms = last_own(groups * shards, bias, queries, cotangent, r6, *state, gain, terms)
    pieces = lax.all_to_all(terms.reshape(groups * shards, 1, BLK), AXES, 0, 0, tiled=True)
    attended = fill_heads(back, out)
    pieces = after(pieces, attended)
    mine = jax.ShapeDtypeStruct((1, 2 * HALF // (groups * shards)), jnp.float32)
    (gain_grad,) = in_vmem(sum_kernel, 0, [mine], pieces.reshape(groups * shards, BLK))
    return attended, gain_grad.reshape(-1)


def solution(mesh):
    placed = (
        P(AXES, None),
        P(AXES, None),
        P(AXES, None),
        P("dp", None),
        P("dp", None, None),
        P("dp", None, None),
        P(),
        P(AXES, None),
    )
    return jax.shard_map(local, mesh=mesh, in_specs=placed, out_specs=(P(AXES, None), P(AXES)), check_vma=False)
```

```python
import functools
import math

import jax
import jax.numpy as jnp
from jax import lax
from jax.experimental import pallas as pl
from jax.experimental.pallas import tpu as pltpu
from jax.sharding import PartitionSpec as P

HEADS = 32
HDIM = 64
REACH = 3
BLK = 128
HALF = HEADS * HDIM // 2
PAIRS = HALF // 128
SENT_AFTER = (3, 6, 8)
NEGATIVE_FILL = -1e30
AXES = ("dp", "seq")


def split_kernel(sides, count, *refs):
    sources, targets, sems = refs[:count], refs[count:-1], refs[-1]
    core = lax.axis_index("seq") % 2
    copies = []
    for side, target in zip(sides, targets):
        columns = pl.ds(pl.multiple_of((core if side == 0 else 1 - core) * HALF, HALF), HALF)
        for part, source in enumerate(sources):
            copy = pltpu.make_async_copy(source.at[:, columns], target.at[cols(part)], sems.at[len(copies)])
            copies.append(copy)
    for copy in copies:
        copy.start()
    for copy in copies:
        copy.wait()


def split_heads(sides, *arrays):
    count = len(sides)
    return pl.pallas_call(
        functools.partial(split_kernel, sides, 2),
        in_specs=[pl.BlockSpec(memory_space=pl.ANY)] * 2,
        out_specs=[pl.BlockSpec(memory_space=pltpu.VMEM)] * count,
        out_shape=[pltpu.VMEM((2 * BLK, HALF), jnp.bfloat16)] * count,
        scratch_shapes=[pltpu.SemaphoreType.DMA((2 * count,))],
        cost_estimate=pl.CostEstimate(flops=0, bytes_accessed=count << 19, transcendentals=0),
    )(*arrays)


OWN, SIB, R1, R2, R3, R4, R5, R6 = range(8)
TILES = (
    [(q, k) for q in (OWN, SIB) for k in (OWN, SIB)]
    + [(q, k) for q in (OWN, SIB) for k in (R1, R2)]
    + [(q, k) for q in (OWN, SIB) for k in (R3, R4)]
    + [(SIB, R5), (OWN, R6)]
)


def key_blocks():
    place = lax.axis_index("seq")
    chip, core = place // 2, place % 2
    toward = 1 - 2 * core
    ring = [(chip, core), (chip, 1 - core)]
    ring += [(chip + toward, core), (chip - toward, 1 - core), (chip - toward, core), (chip + toward, 1 - core)]
    ring += [(chip + 2 * toward, core), (chip - 2 * toward, 1 - core)]
    return [2 * at + side for at, side in ring]


def mask_kernel(keep_ref, docs_ref, links_ref, bias_ref):
    docs_in_pack = links_ref.shape[1]
    nblk = docs_ref.shape[1] // BLK
    blocks = key_blocks()
    target = lax.broadcasted_iota(jnp.int32, (docs_in_pack, docs_in_pack), 1)
    source = lax.broadcasted_iota(jnp.int32, (docs_in_pack, docs_in_pack), 0)
    links = links_ref[0]
    linked = target == links[:, 0:1]
    for at in range(1, links.shape[1]):
        linked = linked | (target == links[:, at : at + 1])
    table = jnp.where(source == target, 2.0, 0.0) + jnp.where(linked, 1.0, 0.0)
    table = table.astype(jnp.bfloat16)

    def one_hot(block):
        at = pl.multiple_of(jnp.clip(block, 0, nblk - 1) * BLK, BLK)
        row = docs_ref[:, pl.ds(at, BLK)]
        rows = lax.broadcasted_iota(jnp.int32, (docs_in_pack, BLK), 0)
        return jnp.where(rows == row, 1.0, 0.0).astype(jnp.bfloat16)

    hots = [one_hot(block) for block in blocks]
    related = [
        lax.dot_general(table, hots[q], (((0,), (0,)), ((), ())), preferred_element_type=jnp.float32).astype(jnp.bfloat16)
        for q in (OWN, SIB)
    ]
    key_at = lax.broadcasted_iota(jnp.int32, (BLK, BLK), 0)
    query_at = lax.broadcasted_iota(jnp.int32, (BLK, BLK), 1)
    apart = query_at - key_at
    for tile, (q, k) in enumerate(TILES):
        query_block, key_block = blocks[q], blocks[k]
        present = (key_block >= 0) & (key_block < nblk)
        kept = keep_ref[0, query_block, jnp.clip(key_block, 0, nblk - 1)] == 1
        least = jnp.where(present, jnp.where(kept, 0.5, 1.5), 9.0)
        relation = lax.dot_general(hots[k], related[q], (((0,), (0,)), ((), ())), preferred_element_type=jnp.float32)
        distance = apart + (query_block - key_block) * BLK
        allowed = (relation > least) & (jnp.abs(distance) <= REACH * BLK)
        bias_ref[tile * BLK : (tile + 1) * BLK] = jnp.where(allowed, 0.0, NEGATIVE_FILL)


def masks(keep, docs, links):
    return in_vmem(mask_kernel, 1, [pltpu.VMEM((len(TILES) * BLK, BLK), jnp.float32)], keep, docs, links, scalars=1)[0]


def absorb(queries, keys, values, biases, state):
    stacked = []
    for query in queries:
        low = lax.broadcasted_iota(jnp.int32, query.shape, 1) < HDIM
        scaled = query * jnp.bfloat16(1.0 / math.sqrt(HDIM))
        nothing = jnp.zeros_like(scaled)
        stacked += [jnp.where(low, scaled, nothing), jnp.where(low, nothing, scaled)]
    scores = lax.dot_general(
        keys, jnp.concatenate(stacked, axis=0), (((1,), (1,)), ((), ())), preferred_element_type=jnp.float32
    )
    scores = scores + jnp.concatenate([bias for bias in biases for _ in range(2)], axis=1)
    largest = jnp.max(scores, axis=0, keepdims=True)
    if state is not None:
        largest = jnp.maximum(state[0], largest)
    expo = jnp.exp(scores - largest)
    totals = jnp.sum(expo, axis=0, keepdims=True)
    sums = lax.dot_general(
        values, expo.astype(jnp.bfloat16), (((0,), (0,)), ((), ())), preferred_element_type=jnp.float32
    )
    folded = fold(sums[:HDIM], sums[HDIM:])
    if state is not None:
        shrink = jnp.exp(state[0] - largest)
        totals = totals + state[1] * shrink
        folded = folded + state[2] * spread(shrink)
    return largest, totals, folded


def fold(first, second):
    blocks = range(0, first.shape[1], 2 * BLK)
    pieces = [jnp.concatenate([first[:, at : at + BLK], second[:, at + BLK : at + 2 * BLK]], axis=0) for at in blocks]
    return jnp.concatenate(pieces, axis=1)


def spread(row):
    wide = jnp.broadcast_to(row, (HDIM, row.shape[1]))
    return fold(wide, wide)


def cols(at):
    return slice(at * BLK, (at + 1) * BLK)


def my_cols(at):
    core = lax.axis_index("seq") % 2
    return pl.ds(pl.multiple_of(core * HALF + at * BLK, BLK), BLK)


def put_state(rows_ref, sums_ref, at, state):
    rows_ref[at * 8 : at * 8 + 1] = state[0]
    rows_ref[at * 8 + 1 : at * 8 + 2] = state[1]
    sums_ref[cols(at)] = state[2]


def get_state(rows_ref, sums_ref, at, first=0, blocks=2):
    of_rows = slice(first * 2 * BLK, (first + blocks) * 2 * BLK)
    of_sums = slice(first * BLK, (first + blocks) * BLK)
    return rows_ref[at * 8 : at * 8 + 1, of_rows], rows_ref[at * 8 + 1 : at * 8 + 2, of_rows], sums_ref[cols(at), of_sums]


def both_kernel(tile, count, bias_ref, query_ref, qc_sib, *refs):
    blocks, before, now = refs[:count], refs[count:-2], refs[-2:]
    for at in range(PAIRS):
        at_cols = cols(at)
        keys = jnp.concatenate([block[:BLK, at_cols] for block in blocks], axis=0)
        values = jnp.concatenate([block[BLK:, at_cols] for block in blocks], axis=0)
        queries = [query_ref[:, my_cols(at)], qc_sib[:BLK, at_cols]]
        biases = [bias_ref[(tile + 2 * side) * BLK : (tile + 2 * side + count) * BLK] for side in range(2)]
        state = get_state(*before, at) if before else None
        put_state(*now, at, absorb(queries, keys, values, biases, state))


def finish(state, gain, cotangent):
    mixed = jnp.transpose(state[2] * spread(1.0 / state[1]))
    attended = (gain * mixed).astype(jnp.bfloat16)
    terms = jnp.sum(mixed * cotangent.astype(jnp.float32), axis=0, keepdims=True)
    return attended, terms


def last(tile, side, at, bias_ref, query, cotangent, kv, rows, sums, gain_ref):
    at_cols = cols(at)
    state = get_state(rows, sums, at, side, 1)
    state = absorb([query], kv[:BLK, at_cols], kv[BLK:, at_cols], [bias_ref[cols(tile)]], state)
    return finish(state, gain_ref[:, my_cols(at)], cotangent)


def sib_kernel(bias_ref, qc, kv, rows, sums, gain_ref, att_ref, terms_ref):
    for at in range(PAIRS):
        query, cotangent = qc[:BLK, cols(at)], qc[BLK:, cols(at)]
        att_ref[:, cols(at)], terms = last(12, 1, at, bias_ref, query, cotangent, kv, rows, sums, gain_ref)
        terms_ref[at : at + 1] = terms


def own_kernel(
    bias_ref, query_ref, cotangent_ref, kv, rows, sums, gain_ref, terms_in, out_ref, terms_ref, att, spread_terms, sems
):
    core = lax.axis_index("seq") % 2
    devices = terms_ref.shape[0] // (2 * PAIRS)
    copies = []

    def send(source, target):
        copies.append(pltpu.make_async_copy(source, target, sems.at[len(copies)]))
        copies[-1].start()

    half = PAIRS * devices
    there = pl.ds(pl.multiple_of((1 - core) * half, half), half)
    spread_terms[there] = jnp.zeros((half, BLK), jnp.float32)
    send(spread_terms.at[there], terms_ref.at[there])
    sent = 0
    for at in range(PAIRS):
        query, cotangent = query_ref[:, my_cols(at)], cotangent_ref[:, my_cols(at)]
        att[:, cols(at)], terms = last(13, 0, at, bias_ref, query, cotangent, kv, rows, sums, gain_ref)
        here = pl.ds(pl.multiple_of((core * PAIRS + at) * devices, devices), devices)
        spread_terms[here] = jnp.broadcast_to(terms + terms_in[at : at + 1], (devices, BLK))
        if at + 1 in SENT_AFTER:
            width = (at + 1 - sent) * BLK
            columns = pl.ds(pl.multiple_of(core * HALF + sent * BLK, BLK), width)
            send(att.at[:, sent * BLK : (at + 1) * BLK], out_ref.at[:, columns])
            place = (core * PAIRS + sent) * devices
            here = pl.ds(pl.multiple_of(place, devices), (at + 1 - sent) * devices)
            send(spread_terms.at[here], terms_ref.at[here])
            sent = at + 1
    for copy in copies:
        copy.wait()


def fill_kernel(back_ref, out_in, out_ref, sem):
    core = lax.axis_index("seq") % 2
    there = pl.ds(pl.multiple_of((1 - core) * HALF, HALF), HALF)
    copy = pltpu.make_async_copy(back_ref, out_ref.at[:, there], sem)
    copy.start()
    copy.wait()


def fill_heads(back, out):
    return pl.pallas_call(
        fill_kernel,
        in_specs=[pl.BlockSpec(memory_space=pltpu.VMEM), pl.BlockSpec(memory_space=pl.ANY)],
        out_specs=pl.BlockSpec(memory_space=pl.ANY),
        out_shape=jax.ShapeDtypeStruct(out.shape, out.dtype),
        input_output_aliases={1: 0},
        scratch_shapes=[pltpu.SemaphoreType.DMA],
        cost_estimate=pl.CostEstimate(flops=0, bytes_accessed=1 << 20, transcendentals=0),
    )(back, out)


STATE = [pltpu.VMEM((PAIRS * 8, 4 * BLK), jnp.float32), pltpu.VMEM((PAIRS * BLK, 2 * BLK), jnp.float32)]


def in_vmem(kernel, tiles, outputs, *operands, scalars=0):
    vmem = pl.BlockSpec(memory_space=pltpu.VMEM)
    smem = pl.BlockSpec(memory_space=pltpu.SMEM)
    cost = pl.CostEstimate(
        flops=tiles * 64 * BLK * BLK * HDIM, bytes_accessed=1 << 20, transcendentals=tiles * 16 * BLK * BLK
    )
    return pl.pallas_call(
        kernel,
        in_specs=[smem] * scalars + [vmem] * (len(operands) - scalars),
        out_specs=[vmem] * len(outputs),
        out_shape=outputs,
        cost_estimate=cost,
        compiler_params=pltpu.CompilerParams(vmem_limit_bytes=8 << 20),
    )(*operands)


def both(tile, bias, queries, qc_sib, blocks, state=()):
    kernel = functools.partial(both_kernel, tile, len(blocks))
    return in_vmem(kernel, 2 * len(blocks), STATE, bias, queries, qc_sib, *blocks, *state)


def last_sib(*operands):
    outputs = [pltpu.VMEM((BLK, HALF), jnp.bfloat16), pltpu.VMEM((PAIRS, BLK), jnp.float32)]
    return in_vmem(sib_kernel, 1, outputs, *operands)


def last_own(devices, *operands):
    return pl.pallas_call(
        own_kernel,
        in_specs=[pl.BlockSpec(memory_space=pltpu.VMEM)] * len(operands),
        out_specs=[pl.BlockSpec(memory_space=pl.ANY)] * 2,
        out_shape=[
            jax.ShapeDtypeStruct((BLK, 2 * HALF), jnp.bfloat16),
            jax.ShapeDtypeStruct((devices, BLK), jnp.float32),
        ],
        scratch_shapes=[
            pltpu.VMEM((BLK, HALF), jnp.bfloat16),
            pltpu.VMEM((devices, BLK), jnp.float32),
            pltpu.SemaphoreType.DMA((1 + 2 * len(SENT_AFTER),)),
        ],
        cost_estimate=pl.CostEstimate(flops=64 * BLK * BLK * HDIM, bytes_accessed=1 << 20, transcendentals=16 * BLK * BLK),
        compiler_params=pltpu.CompilerParams(vmem_limit_bytes=8 << 20),
    )(*operands)


def sum_kernel(pieces_ref, out_ref):
    mine = out_ref.shape[1]
    place = lax.axis_index("dp") * lax.axis_size("seq") + lax.axis_index("seq")
    total = jnp.sum(pieces_ref[...], axis=0, keepdims=True)
    at = lax.rem(place, BLK // mine) * mine
    out_ref[...] = pltpu.roll(total, lax.rem(BLK - at, BLK), 1)[:, :mine]


def rotations(groups, shards):
    onward = []
    for group in range(groups):
        for place in range(shards):
            chip, core = divmod(place, 2)
            there = chip + (1 if core == 1 else -1)
            target = there * 2 + core if 0 <= there < shards // 2 else chip * 2 + 1 - core
            onward.append((group * shards + place, group * shards + target))
    backward = [(target, source) for source, target in onward]
    crossing = lambda ring: [(at, to ^ 1 if to // 2 != at // 2 else at) for at, to in ring]
    return onward, backward, crossing(onward), crossing(backward)


def after(value, *others):
    return lax.optimization_barrier((value, *others))[0]


def local(queries, key_rows, value_rows, document_ids, link_lists, block_keep, out_gain, cotangent):
    groups, shards = lax.axis_size("dp"), lax.axis_size("seq")
    onward, backward, outward, inward = rotations(groups, shards)
    siblings = [(i, i ^ 1) for i in range(groups * shards)]
    move = lambda value, pairs: lax.ppermute(value, AXES, pairs)
    gain = out_gain.reshape(1, -1)

    kv_own, kv_send = split_heads((0, 1), key_rows, value_rows)
    r1 = move(kv_own, onward)
    r2 = move(kv_send, outward)
    kv_sib = move(kv_send, siblings)
    (qc_send,) = split_heads((1,), after(queries, kv_sib), cotangent)
    qc_sib = move(qc_send, siblings)
    r3 = move(after(kv_own, kv_sib), backward)
    r4 = move(after(kv_send, qc_sib), inward)
    r5 = move(r1, onward)
    bias = masks(block_keep, after(document_ids, kv_sib), link_lists)
    state = both(0, bias, queries, qc_sib, (kv_own, kv_sib))
    r6 = move(after(r2, *state), backward)
    state = both(4, bias, queries, qc_sib, (r1, r2), state)
    state = both(8, bias, queries, qc_sib, (r3,), state)
    state = both(9, bias, queries, qc_sib, (r4,), state)
    att_sib, terms = last_sib(bias, qc_sib, r5, *state, gain)
    back = move(att_sib, siblings)
    out, terms = last_own(groups * shards, bias, queries, cotangent, r6, *state, gain, terms)
    pieces = lax.all_to_all(terms.reshape(groups * shards, 1, BLK), AXES, 0, 0, tiled=True)
    attended = fill_heads(back, out)
    pieces = after(pieces, attended)
    mine = jax.ShapeDtypeStruct((1, 2 * HALF // (groups * shards)), jnp.float32)
    (gain_grad,) = in_vmem(sum_kernel, 0, [mine], pieces.reshape(groups * shards, BLK))
    return attended, gain_grad.reshape(-1)


def solution(mesh):
    placed = (
        P(AXES, None),
        P(AXES, None),
        P(AXES, None),
        P("dp", None),
        P("dp", None, None),
        P("dp", None, None),
        P(),
        P(AXES, None),
    )
    return jax.shard_map(local, mesh=mesh, in_specs=placed, out_specs=(P(AXES, None), P(AXES)), check_vma=False)
```
